256 devices in a mesh: tm: 4 (over y), ha: 16 (over z, core), wa: 4 (over x).
Axes of the slice: x: 4, y: 4, z: 8, core: 2. Of those that a mesh axis runs over, the one named last changes fastest.
Arguments:
- features: bfloat16 [4, 32, 512, 512], P('tm', 'ha', 'wa'), may hold values from -100 to 100
- gain_one: float32 [512], replicated, may hold values from 0.1 to 1.9
- shift_one: float32 [512], replicated, may hold values from -3 to 3
- conv_weight: bfloat16 [3, 3, 3, 512, 512], P(None, None, None, None, 'wa'), may hold values from -0.0546875 to 0.0546875
- gain_two: float32 [512], replicated, may hold values from 0.1 to 1.9
- shift_two: float32 [512], replicated, may hold values from -3 to 3
Outputs:
- block_out: bfloat16 [4, 32, 512, 512], P('tm', 'ha', 'wa')
The draws below stay inside these ranges and needn't reach their ends.
All inputs are finite; a program needn't handle non-finite values.
Results may differ from the reference program's by a relative error of at most 0.012.
Values may be sent and summed in bfloat16 or wider, within the bound.
A program may use at most 128 MiB of HBM per device.

```python
import math
import jax
import jax.numpy as jnp
from jax import lax

C = 512
GROUPS = 32
NF = 4
NH = 32
NW = 512


def draw_features(key, part):
    key = jax.random.fold_in(key, 11)
    base_key, row_key, column_key, channel_key = jax.random.split(key, 4)
    frame_pos = jnp.arange(NF, dtype=jnp.float32) / max(NF - 1, 1)
    height_pos = jnp.arange(NH, dtype=jnp.float32) / max(NH - 1, 1)
    width_pos = jnp.arange(NW, dtype=jnp.float32) / max(NW - 1, 1)
    trend = 3.0 ** (frame_pos[:, None, None] + height_pos[None, :, None] + width_pos[None, None, :])
    row_scale = jnp.exp(jax.random.uniform(row_key, (NF, NH, 1), jnp.float32, 0.0, 0.5 * math.log(10.0)))
    column_scale = jnp.exp(jax.random.uniform(column_key, (1, 1, NW), jnp.float32, 0.0, 0.5 * math.log(10.0)))
    channel_scale = jnp.exp(jax.random.uniform(channel_key, (C,), jnp.float32, math.log(0.5), math.log(2.0)))
    base = jnp.clip(jax.random.normal(base_key, (NF, NH, NW, C), jnp.float32), -4.0, 4.0)
    values = base * (trend * row_scale * column_scale)[..., None] * channel_scale * 0.1
    return jnp.clip(values, -100.0, 100.0).astype(jnp.bfloat16)


def level_of(rng, extent, pieces, least, top_value):
    gain, own = 1.0, jax.random.fold_in(rng, 6)
    for position, parts in pieces:
        heights = jnp.exp(jax.random.uniform(jax.random.fold_in(own, position), (parts,), jnp.float32, least / len(pieces), top_value / len(pieces)))
        gain = gain * jnp.repeat(heights, extent[position] // parts).reshape([-1 if axis == position else 1 for axis in range(len(extent))])
    return gain


def normal_values(key, dims, scale, bound, cuts=(), kind=jnp.bfloat16):
    level = level_of(key, dims, cuts, -0.22, 0.18) if cuts else 1.0
    drawn = jax.random.normal(key, dims, jnp.float32) * scale * level
    return jnp.minimum(jnp.maximum(drawn, -bound), bound).astype(kind)


def setup_inputs(seed: int = 0) -> dict:
    key_list = jax.random.split(jax.random.key(seed), 7)
    features = draw_features(jax.random.fold_in(key_list[6], 71), 0)
    gain_one = jnp.clip(1.0 + 0.18 * jax.random.normal(key_list[1], (C,), jnp.float32), 0.1, 1.9)
    shift_one = normal_values(key_list[2], (C,), 0.5, 3.0, (), jnp.float32)
    conv_weight = normal_values(key_list[3], (3, 3, 3, C, C), (27 * C) ** -0.5, 0.0546875, ((4, 4),))
    gain_two = jnp.clip(1.0 + 0.18 * jax.random.normal(key_list[4], (C,), jnp.float32), 0.1, 1.9)
    shift_two = normal_values(key_list[5], (C,), 0.5, 3.0, (), jnp.float32)
    return dict(features=features, gain_one=gain_one, shift_one=shift_one, conv_weight=conv_weight, gain_two=gain_two, shift_two=shift_two)


def normalize(values, gain_vector, offset_vector):
    grouped = values.reshape(NF, NH, NW, GROUPS, C // GROUPS)
    group_mean = lax.optimization_barrier(jnp.mean(grouped, axis=(0, 1, 2, 4)))
    centered = grouped - group_mean[:, None]
    group_var = lax.optimization_barrier(jnp.mean(centered * centered, axis=(0, 1, 2, 4)))
    scaled = centered * lax.rsqrt(group_var + 1e-06)[:, None]
    return scaled.reshape(NF, NH, NW, C) * gain_vector + offset_vector

def reference(features, gain_one, shift_one, conv_weight, gain_two, shift_two):
    activated = jax.nn.silu(normalize(features.astype(jnp.float32), gain_one, shift_one)).astype(jnp.bfloat16)
    padded = jnp.pad(activated, ((2, 0), (1, 1), (1, 1), (0, 0)), mode='edge')
    outputs = []
    for frame_index in range(NF):
        accumulated = jnp.zeros((NH * NW, C), jnp.float32)
        for depth_tap in range(3):
            for row_tap in range(3):
                for col_tap in range(3):
                    window = padded[frame_index + depth_tap, row_tap:row_tap + NH, col_tap:col_tap + NW].reshape(NH * NW, C)
                    accumulated = accumulated + jnp.dot(window, conv_weight[depth_tap, row_tap, col_tap], preferred_element_type=jnp.float32)
        outputs.append(accumulated.reshape(1, NH, NW, C))
    convolved = jnp.concatenate(outputs, axis=0)
    return jax.nn.silu(normalize(convolved, gain_two, shift_two)).astype(jnp.bfloat16)
```

```python
import functools

import jax
import jax.numpy as jnp
from jax import lax
from jax.experimental import pallas as pl
from jax.experimental.pallas import tpu as pltpu
from jax.sharding import PartitionSpec as P

GROUPS = 32
LANES = 128
EPS = 1e-06
MESH = pl.DeviceIdType.MESH


def lane_blocks(rows):
    return [rows[k : k + 1, :] for k in range(rows.shape[0])]


def group_sum(values, width):
    axis = values.ndim - 1
    lane = lax.broadcasted_iota(jnp.int32, values.shape, axis)
    step = 1
    while step < width:
        ahead = pltpu.roll(values, step, axis)
        behind = pltpu.roll(values, LANES - step, axis)
        values = values + jnp.where((lane & step) != 0, ahead, behind)
        step *= 2
    return values


def combined(means, deviations, count, axis):
    mean = jnp.mean(means, axis=axis, keepdims=True)
    spread = means - mean
    total = jnp.sum(deviations, axis=axis) + count * jnp.sum(spread * spread, axis=axis)
    return jnp.squeeze(mean, axis), total


def group_norm_terms(mean, deviation, count, width):
    group_mean = group_sum(mean, width) / width
    spread = mean - group_mean
    group_var = group_sum(deviation + count * (spread * spread), width) / (count * width)
    return group_mean, lax.rsqrt(group_var + EPS)


def silu(v):
    half = 0.5 * v
    return half + half * jnp.tanh(half)


def kernel(
    nt, nh, nw,
    feat, gain_one, shift_one, weight, gain_two, shift_two, out,
    edge_out, blocks, edges, acts, pair_a, pair_b, rims, acc, conv, conv_out, rim_out, rim_in, back,
    plane_one, line_one, line_two, plane_two, norm, norm_edge,
    weight_sem, local_sem, send_sem, recv_sem, rim_send, rim_recv,
):
    t, h, w = lax.axis_index("tm"), lax.axis_index("ha"), lax.axis_index("wa")
    plane = nt * nw
    me = t * nw + w
    columns, channels = feat.shape[2], feat.shape[3]
    part = columns // nt
    blocks_of = channels // LANES
    width = channels // GROUPS
    depth = 3 * channels
    span = nw * part
    rows = nt * span
    entries = 2 * columns
    everywhere = entries * plane * nh

    def plane_id(j):
        return (lax.div(j, nw), h, lax.rem(j, nw))

    def plane_loop(body):
        def step(i, carry):
            body(lax.rem(me + i, plane))
            return carry

        lax.fori_loop(1, plane, step, 0)

    def line_loop(body):
        def step(i, carry):
            body(lax.rem(h + i, nh))
            return carry

        lax.fori_loop(1, nh, step, 0)

    barrier = pltpu.get_barrier_semaphore()

    def greet(device):
        pl.semaphore_signal(barrier, inc=1, device_id=device, device_id_type=MESH)

    plane_loop(lambda j: greet(plane_id(j)))
    line_loop(lambda j: greet((t, j, w)))

    above = jnp.where(h == 0, 0, 2)
    below = jnp.where(h == nh - 1, 2, 0)
    left_half, right_half = pl.ds(0, LANES), pl.ds(LANES, LANES)
    weight_copies = []
    for k in range(3):
        weight_copies += [
            (weight.at[k, above], rims.at[0, k]),
            (weight.at[k, below], rims.at[1, k]),
            (weight.at[k, 1], pair_a.at[k, :, left_half]),
            (weight.at[k, 0], pair_a.at[k, :, right_half]),
            (weight.at[k, 2], pair_b.at[k, :, left_half]),
            (weight.at[k, 1], pair_b.at[k, :, right_half]),
        ]
    weight_copies = [
        pltpu.make_async_copy(source, target, weight_sem.at[n])
        for n, (source, target) in enumerate(weight_copies)
    ]
    for copy in weight_copies:
        copy.start()

    values = feat[0].astype(jnp.float32)
    flat = values.reshape(entries, channels)
    mean = jnp.mean(flat, axis=0, keepdims=True)
    centered = flat - mean
    deviation = jnp.sum(centered * centered, axis=0, keepdims=True)
    plane_one[me] = jnp.zeros((8, LANES), jnp.float32)
    for k in range(blocks_of):
        lanes = slice(k * LANES, (k + 1) * LANES)
        plane_one[me, k : k + 1, :] = mean[:, lanes]
        plane_one[me, 4 + k : 5 + k, :] = deviation[:, lanes]
    for y in range(nt):
        left = (y * part - 1) % columns
        right = (y * part + part) % columns
        four = jnp.concatenate(
            [values[r, c : c + 1, :] for c in (left, right) for r in range(2)], axis=0
        )
        pieces = [four[:, k * LANES : (k + 1) * LANES] for k in range(blocks_of)]
        pieces += [jnp.zeros((4, LANES), jnp.float32)] * (4 - blocks_of)
        edge_out[y] = jnp.concatenate(pieces, axis=0).astype(jnp.bfloat16)

    own_block = pltpu.make_async_copy(feat.at[0, :, pl.ds(t * part, part), :], blocks.at[me], local_sem.at[0])
    own_edge = pltpu.make_async_copy(edge_out.at[t], edges.at[me], local_sem.at[1])
    own_block.start()
    own_edge.start()

    pl.semaphore_wait(barrier, plane - 1 + nh - 1)

    def remote(source, target, index, device):
        return pltpu.make_async_remote_copy(
            src_ref=source, dst_ref=target, send_sem=send_sem.at[index], recv_sem=recv_sem.at[index],
            device_id=device, device_id_type=MESH,
        )

    def all_arrived(buffer, index):
        pltpu.make_async_copy(buffer, buffer, recv_sem.at[index]).wait()

    def all_sent(buffer, index):
        pltpu.make_async_copy(buffer, buffer, send_sem.at[index]).wait()

    plane_loop(lambda j: remote(plane_one.at[me], plane_one.at[me], 0, plane_id(j)).start())

    def send_block(j):
        y = lax.div(j, nw)
        remote(feat.at[0, :, pl.ds(y * part, part), :], blocks.at[me], 1, plane_id(j)).start()
        remote(edge_out.at[y], edges.at[me], 2, plane_id(j)).start()

    plane_loop(send_block)

    others = pl.ds(0, plane - 1)
    all_arrived(plane_one.at[others], 0)
    all_sent(plane_one.at[others], 0)
    mean, deviation = combined(plane_one[:, 0:4, :], plane_one[:, 4:8, :], float(entries), 0)
    line_one[h] = jnp.concatenate([mean, deviation], axis=0)
    line_loop(lambda j: remote(line_one.at[h], line_one.at[h], 3, (t, j, w)).start())
    all_arrived(line_one.at[pl.ds(0, nh - 1)], 3)
    all_sent(line_one.at[pl.ds(0, nh - 1)], 3)
    mean, deviation = combined(line_one[:, 0:4, :], line_one[:, 4:8, :], float(entries * plane), 0)
    mean, inverse = group_norm_terms(mean, deviation, float(everywhere), float(width))
    wide_mean = jnp.concatenate(lane_blocks(mean[0:blocks_of]), axis=1)
    wide_scale = jnp.concatenate(lane_blocks(inverse[0:blocks_of]), axis=1) * gain_one[...]
    norm[0:1, :] = wide_mean
    norm[1:2, :] = wide_scale
    norm[2:3, :] = shift_one[...]
    for n, vector in enumerate((wide_mean, wide_scale, shift_one[...])):
        for k in range(blocks_of):
            norm_edge[n, 4 * k : 4 * k + 4, :] = jnp.broadcast_to(
                vector[:, k * LANES : (k + 1) * LANES], (4, LANES)
            )
        if blocks_of < 4:
            norm_edge[n, 4 * blocks_of :, :] = jnp.zeros((16 - 4 * blocks_of, LANES), jnp.float32)

    all_arrived(blocks.at[others], 1)
    all_arrived(edges.at[others], 2)
    own_block.wait()
    own_edge.wait()

    first = lax.broadcasted_iota(jnp.int32, (part, channels), 0) == 0
    last = lax.broadcasted_iota(jnp.int32, (part, channels), 0) == part - 1
    is_left = (lax.broadcasted_iota(jnp.int32, (16, LANES), 0) & 2) == 0

    def activate(j, carry):
        frame, block = lax.div(j, nw), lax.rem(j, nw)
        left_from = jnp.where(t == 0, jnp.maximum(block - 1, 0), block)
        right_from = jnp.where(t == nt - 1, jnp.minimum(block + 1, nw - 1), block)
        left_end = jnp.logical_and(t == 0, block == 0)
        right_end = jnp.logical_and(t == nt - 1, block == nw - 1)
        edge = jnp.where(
            is_left,
            edges[frame * nw + left_from].astype(jnp.float32),
            edges[frame * nw + right_from].astype(jnp.float32),
        )
        edge = silu((edge - norm_edge[0]) * norm_edge[1] + norm_edge[2])
        for r in range(2):
            middle = silu((blocks[j, r].astype(jnp.float32) - norm[0:1, :]) * norm[1:2, :] + norm[2:3, :])
            left = jnp.concatenate([edge[4 * k + r : 4 * k + r + 1] for k in range(blocks_of)], axis=1)
            right = jnp.concatenate([edge[4 * k + 2 + r : 4 * k + 3 + r] for k in range(blocks_of)], axis=1)
            left = jnp.where(left_end, middle[0:1, :], left)
            right = jnp.where(right_end, middle[part - 1 : part, :], right)
            before = jnp.where(first, left, pltpu.roll(middle, 1, 0)).astype(jnp.bfloat16)
            after = jnp.where(last, right, pltpu.roll(middle, part - 1, 0)).astype(jnp.bfloat16)
            middle = middle.astype(jnp.bfloat16)

            def put(slot, before=before, middle=middle, after=after, r=r):
                place = pl.ds(pl.multiple_of(slot * span + block * part, part), part)
                acts[r, place, 0:channels] = before
                acts[r, place, channels : 2 * channels] = middle
                acts[r, place, 2 * channels : 3 * channels] = after

            put(frame + 2)

            @pl.when(frame == 0)
            def _(put=put):
                put(0)
                put(1)

        return carry

    lax.fori_loop(0, plane, activate, 0)

    for copy in weight_copies:
        copy.wait()

    def window(r, k):
        return acts[r, pl.ds(pl.multiple_of(k * span, span), rows), :]

    for side in range(2):
        acc[:, left_half] = jnp.zeros((rows, LANES), jnp.float32)

        def rim_step(k, carry, side=side):
            acc[:, left_half] += jnp.dot(window(side, k), rims[side, k], preferred_element_type=jnp.float32)
            return carry

        lax.fori_loop(0, 3, rim_step, 0)
        rim_out[side] = acc[:, left_half].astype(jnp.bfloat16)

        at_end = (h == 0) if side == 0 else (h == nh - 1)

        @pl.when(at_end)
        def _(side=side):
            rim_in[side] = rim_out[side]

        @pl.when(jnp.logical_not(at_end))
        def _(side=side):
            pltpu.make_async_remote_copy(
                src_ref=rim_out.at[side], dst_ref=rim_in.at[1 - side],
                send_sem=rim_send.at[side], recv_sem=rim_recv.at[1 - side],
                device_id=(t, h - 1 if side == 0 else h + 1, w), device_id_type=MESH,
            ).start()

    acc[...] = jnp.zeros((rows, 2 * LANES), jnp.float32)

    def pair_step(k, carry):
        acc[...] += jnp.dot(window(0, k), pair_a[k], preferred_element_type=jnp.float32) + jnp.dot(
            window(1, k), pair_b[k], preferred_element_type=jnp.float32
        )
        return carry

    lax.fori_loop(0, 3, pair_step, 0)

    for side in range(2):
        at_end = (h == 0) if side == 0 else (h == nh - 1)

        @pl.when(jnp.logical_not(at_end))
        def _(side=side):
            pltpu.make_async_copy(rim_in.at[side], rim_in.at[side], rim_recv.at[side]).wait()
            pltpu.make_async_copy(rim_out.at[side], rim_out.at[side], rim_send.at[side]).wait()

    sums = jnp.zeros((1, LANES), jnp.float32)
    for r in range(2):
        total = acc[:, r * LANES : (r + 1) * LANES] + rim_in[r].astype(jnp.float32)
        conv[r] = total
        conv_out[r] = total.astype(jnp.bfloat16)
        sums = sums + jnp.sum(total, axis=0, keepdims=True)
    mean = sums / (2 * rows)
    deviation = jnp.zeros((1, LANES), jnp.float32)
    for r in range(2):
        centered = conv[r] - mean
        deviation = deviation + jnp.sum(centered * centered, axis=0, keepdims=True)
    line_two[h] = jnp.zeros((8, LANES), jnp.float32)
    line_two[h, 0:1, :] = mean
    line_two[h, 1:2, :] = deviation
    line_loop(lambda j: remote(line_two.at[h], line_two.at[h], 4, (t, j, w)).start())

    def block_rows(j):
        return conv_out.at[:, pl.ds(pl.multiple_of(j * part, part), part), :]

    own_place = back.at[:, pl.ds(t * part, part), pl.ds(pl.multiple_of(w * LANES, LANES), LANES)]
    plane_loop(lambda j: remote(block_rows(j), own_place, 5, plane_id(j)).start())
    own_back = pltpu.make_async_copy(block_rows(me), own_place, local_sem.at[0])
    own_back.start()

    all_arrived(line_two.at[pl.ds(0, nh - 1)], 4)
    all_sent(line_two.at[pl.ds(0, nh - 1)], 4)
    mean, deviation = combined(line_two[:, 0:1, :], line_two[:, 1:2, :], float(2 * rows), 0)
    plane_two[me] = jnp.zeros((8, LANES), jnp.float32)
    plane_two[me, 0:1, :] = mean
    plane_two[me, 1:2, :] = deviation
    plane_loop(lambda j: remote(plane_two.at[me], plane_two.at[me], 6, plane_id(j)).start())
    all_arrived(plane_two.at[others], 6)
    all_sent(plane_two.at[others], 6)
    gathered = plane_two[...].reshape(nt, nw, 8, LANES)
    mean, deviation = combined(gathered[:, :, 0, :], gathered[:, :, 1, :], float(2 * rows * nh), 0)
    mean, inverse = group_norm_terms(mean, deviation, float(everywhere), float(width))
    norm[0:1, :] = jnp.concatenate(lane_blocks(mean), axis=1)
    norm[1:2, :] = jnp.concatenate(lane_blocks(inverse), axis=1) * gain_two[...]
    norm[2:3, :] = shift_two[...]

    arrived_rows = conv_out.at[:, pl.ds(0, (plane - 1) * part), :]
    all_arrived(arrived_rows, 5)
    own_back.wait()
    for r in range(2):
        out[0, r] = silu(
            (back[r].astype(jnp.float32) - norm[0:1, :]) * norm[1:2, :] + norm[2:3, :]
        ).astype(jnp.bfloat16)

    all_sent(arrived_rows, 5)
    all_sent(blocks.at[others], 1)
    all_sent(edges.at[others], 2)


def solution(mesh):
    nt, nh, nw = mesh.shape["tm"], mesh.shape["ha"], mesh.shape["wa"]

    def per_device(features, gain_one, shift_one, conv_weight, gain_two, shift_two):
        columns, channels = features.shape[2], features.shape[3]
        own = conv_weight.shape[4]
        plane, part, depth = nt * nw, columns // nt, 3 * channels
        span = nw * part
        rows = nt * span
        vmem = pl.BlockSpec(memory_space=pltpu.VMEM)
        bf16, f32 = jnp.bfloat16, jnp.float32
        return pl.pallas_call(
            functools.partial(kernel, nt, nh, nw),
            out_shape=jax.ShapeDtypeStruct(features.shape, bf16),
            in_specs=[vmem, vmem, vmem, pl.BlockSpec(memory_space=pl.ANY), vmem, vmem],
            out_specs=vmem,
            scratch_shapes=[
                pltpu.VMEM((nt, 16, LANES), bf16),
                pltpu.VMEM((plane, 2, part, channels), bf16),
                pltpu.VMEM((plane, 16, LANES), bf16),
                pltpu.VMEM((2, (nt + 2) * span, depth), bf16),
                pltpu.VMEM((3, depth, 2 * own), bf16),
                pltpu.VMEM((3, depth, 2 * own), bf16),
                pltpu.VMEM((2, 3, depth, own), bf16),
                pltpu.VMEM((rows, 2 * own), f32),
                pltpu.VMEM((2, rows, own), f32),
                pltpu.VMEM((2, rows, own), bf16),
                pltpu.VMEM((2, rows, own), bf16),
                pltpu.VMEM((2, rows, own), bf16),
                pltpu.VMEM((2, columns, channels), bf16),
                pltpu.VMEM((plane, 8, LANES), f32),
                pltpu.VMEM((nh, 8, LANES), f32),
                pltpu.VMEM((nh, 8, LANES), f32),
                pltpu.VMEM((plane, 8, LANES), f32),
                pltpu.VMEM((8, channels), f32),
                pltpu.VMEM((3, 16, LANES), f32),
                pltpu.SemaphoreType.DMA((18,)),
                pltpu.SemaphoreType.DMA((2,)),
                pltpu.SemaphoreType.DMA((7,)),
                pltpu.SemaphoreType.DMA((7,)),
                pltpu.SemaphoreType.DMA((2,)),
                pltpu.SemaphoreType.DMA((2,)),
            ],
            compiler_params=pltpu.CompilerParams(
                collective_id=0, has_side_effects=True, vmem_limit_bytes=48 * 1024 * 1024
            ),
        )(
            features,
            gain_one.reshape(1, channels),
            shift_one.reshape(1, channels),
            conv_weight.reshape(3, 3, depth, own),
            gain_two.reshape(1, channels),
            shift_two.reshape(1, channels),
        )

    in_specs = (P("tm", "ha", "wa", None), P(), P(), P(None, None, None, None, "wa"), P(), P())
    return jax.shard_map(
        per_device, mesh=mesh, in_specs=in_specs, out_specs=P("tm", "ha", "wa", None), check_vma=False
    )
```

```python
import functools

import jax
import jax.numpy as jnp
from jax import lax
from jax.experimental import pallas as pl
from jax.experimental.pallas import tpu as pltpu
from jax.sharding import PartitionSpec as P

GROUPS = 32
LANES = 128
EPS = 1e-06
MESH = pl.DeviceIdType.MESH


def lane_blocks(rows):
    return [rows[k : k + 1, :] for k in range(rows.shape[0])]


def group_sum(values, width):
    axis = values.ndim - 1
    lane = lax.broadcasted_iota(jnp.int32, values.shape, axis)
    step = 1
    while step < width:
        ahead = pltpu.roll(values, step, axis)
        behind = pltpu.roll(values, LANES - step, axis)
        values = values + jnp.where((lane & step) != 0, ahead, behind)
        step *= 2
    return values


def combined(means, deviations, count, axis):
    mean = jnp.mean(means, axis=axis, keepdims=True)
    spread = means - mean
    total = jnp.sum(deviations, axis=axis) + count * jnp.sum(spread * spread, axis=axis)
    return jnp.squeeze(mean, axis), total


def group_norm_terms(mean, deviation, count, width):
    group_mean = group_sum(mean, width) / width
    spread = mean - group_mean
    group_var = group_sum(deviation + count * (spread * spread), width) / (count * width)
    return group_mean, lax.rsqrt(group_var + EPS)


def silu(v):
    half = 0.5 * v
    return half + half * jnp.tanh(half)


def hops(distance, count):
    return min(distance, count - distance)


def kernel(
    nt, nh, nw,
    feat_hbm, gain_one_hbm, shift_one_hbm, weight, gain_two_hbm, shift_two_hbm, out,
    feat, gain_one, shift_one, gain_two, shift_two,
    message, blocks, acts, pair_a, pair_b, rim_pair, rim_last, acc, conv, conv_out, rim_out, rim_in, back,
    plane_one, line_one, line_two, plane_two, norm, norm_edge,
    input_sem, weight_sem, local_sem, send_sem, recv_sem, rim_send, rim_recv,
):
    t, h, w = lax.axis_index("tm"), lax.axis_index("ha"), lax.axis_index("wa")
    plane = nt * nw
    me = t * nw + w
    columns, channels = feat.shape[2], feat.shape[3]
    part = columns // nt
    blocks_of = channels // LANES
    width = channels // GROUPS
    depth = 3 * channels
    span = nw * part
    rows = nt * span
    entries = 2 * columns
    everywhere = entries * plane * nh
    slots = sorted(range(nw), key=lambda d: d % 2)
    near = nw // 2
    offsets = [(a, b) for a in range(nt) for b in range(nw) if a or b]
    far_first = sorted(offsets, key=lambda d: -hops(d[0], nt) - hops(d[1], nw))

    def plane_peer(offset):
        return lax.rem(t + offset[0], nt), lax.rem(w + offset[1], nw)

    def line_loop(body):
        def step(i, carry):
            away = lax.div(i + 1, 2)
            offset = nh // 2 + jnp.where(lax.rem(i, 2) == 1, away, -away)
            body(lax.rem(h + offset, nh))
            return carry

        lax.fori_loop(0, nh - 1, step, 0)

    copy_in = [
        pltpu.make_async_copy(source, target, input_sem.at[n])
        for n, (source, target) in enumerate(
            (
                (feat_hbm, feat),
                (gain_one_hbm, gain_one),
                (shift_one_hbm, shift_one),
                (gain_two_hbm, gain_two),
                (shift_two_hbm, shift_two),
            )
        )
    ]
    copy_in[0].start()

    barrier = pltpu.get_barrier_semaphore()

    def greet(device):
        pl.semaphore_signal(barrier, inc=1, device_id=device, device_id_type=MESH)

    line_loop(lambda j: greet((t, j, w)))
    for offset in far_first:
        y, q = plane_peer(offset)
        greet((y, h, q))

    for copy in copy_in[1:]:
        copy.start()
    above = jnp.where(h == 0, 0, 2)
    below = jnp.where(h == nh - 1, 2, 0)
    left_half, right_half = pl.ds(0, LANES), pl.ds(LANES, LANES)
    weight_copies = []
    for side, row in ((0, above), (1, below)):
        weight_copies += [
            (weight.at[0, row], rim_pair.at[side, :, left_half]),
            (weight.at[1, row], rim_pair.at[side, :, right_half]),
            (weight.at[2, row], rim_last.at[side]),
        ]
    for k in range(3):
        weight_copies += [
            (weight.at[k, 1], pair_a.at[k, :, left_half]),
            (weight.at[k, 0], pair_a.at[k, :, right_half]),
            (weight.at[k, 2], pair_b.at[k, :, left_half]),
            (weight.at[k, 1], pair_b.at[k, :, right_half]),
        ]
    weight_copies = [
        pltpu.make_async_copy(source, target, weight_sem.at[n])
        for n, (source, target) in enumerate(weight_copies)
    ]

    copy_in[0].wait()
    for copy in weight_copies:
        copy.start()
    values = feat[0].astype(jnp.float32)
    flat = values.reshape(entries, channels)
    mean = jnp.mean(flat, axis=0, keepdims=True)
    centered = flat - mean
    deviation = jnp.sum(centered * centered, axis=0, keepdims=True)
    pieces = [mean[:, k * LANES : (k + 1) * LANES] for k in range(blocks_of)]
    pieces += [jnp.zeros((1, LANES), jnp.float32)] * (4 - blocks_of)
    pieces += [deviation[:, k * LANES : (k + 1) * LANES] for k in range(blocks_of)]
    pieces += [jnp.zeros((1, LANES), jnp.float32)] * (4 - blocks_of)
    local_terms = jnp.concatenate(pieces, axis=0)
    for y in range(nt):
        left = (y * part - 1) % columns
        right = (y * part + part) % columns
        four = jnp.concatenate(
            [values[r, c : c + 1, :] for c in (left, right) for r in range(2)], axis=0
        )
        pieces = [four[:, k * LANES : (k + 1) * LANES] for k in range(blocks_of)]
        pieces += [jnp.zeros((4, LANES), jnp.float32)] * (4 - blocks_of)
        message[y, 8:24, :] = jnp.concatenate(pieces, axis=0)
    line_one[h] = local_terms

    own_block = pltpu.make_async_copy(feat.at[0, :, pl.ds(t * part, part), :], blocks.at[me], local_sem.at[0])
    own_block.start()

    pl.semaphore_wait(barrier, plane - 1 + nh - 1)

    def remote(source, target, index, device):
        return pltpu.make_async_remote_copy(
            src_ref=source, dst_ref=target, send_sem=send_sem.at[index], recv_sem=recv_sem.at[index],
            device_id=device, device_id_type=MESH,
        )

    def all_arrived(buffer, index):
        pltpu.make_async_copy(buffer, buffer, recv_sem.at[index]).wait()

    def all_sent(buffer, index):
        pltpu.make_async_copy(buffer, buffer, send_sem.at[index]).wait()

    def send_blocks(stage):
        for offset in far_first:
            if (slots.index(offset[1]) >= near) == stage:
                y, q = plane_peer(offset)
                remote(feat.at[0, :, pl.ds(y * part, part), :], blocks.at[me], 1 + stage, (y, h, q)).start()

    line_loop(lambda j: remote(line_one.at[h], line_one.at[h], 3, (t, j, w)).start())
    send_blocks(0)
    others = pl.ds(0, plane - 1)
    all_arrived(line_one.at[pl.ds(0, nh - 1)], 3)
    mean, deviation = combined(line_one[:, 0:4, :], line_one[:, 4:8, :], float(entries), 0)
    combined_terms = jnp.concatenate([mean, deviation], axis=0)
    for y in range(nt):
        message[y, 0:8, :] = combined_terms
    for offset in far_first:
        y, q = plane_peer(offset)
        remote(message.at[y], plane_one.at[me], 0, (y, h, q)).start()
    send_blocks(1)
    plane_one[me] = message[t]
    for copy in copy_in[1:]:
        copy.wait()
    for copy in weight_copies:
        copy.wait()
    all_arrived(plane_one.at[others], 0)
    mean, deviation = combined(plane_one[:, 0:4, :], plane_one[:, 4:8, :], float(entries * nh), 0)
    mean, inverse = group_norm_terms(mean, deviation, float(everywhere), float(width))
    wide_mean = jnp.concatenate(lane_blocks(mean[0:blocks_of]), axis=1)
    wide_scale = jnp.concatenate(lane_blocks(inverse[0:blocks_of]), axis=1) * gain_one[...]
    norm[0:1, :] = wide_mean
    norm[1:2, :] = wide_scale
    norm[2:3, :] = shift_one[...]
    for n, vector in enumerate((wide_mean, wide_scale, shift_one[...])):
        for k in range(blocks_of):
            norm_edge[n, 4 * k : 4 * k + 4, :] = jnp.broadcast_to(
                vector[:, k * LANES : (k + 1) * LANES], (4, LANES)
            )
        if blocks_of < 4:
            norm_edge[n, 4 * blocks_of :, :] = jnp.zeros((16 - 4 * blocks_of, LANES), jnp.float32)

    first = lax.broadcasted_iota(jnp.int32, (part, channels), 0) == 0
    last = lax.broadcasted_iota(jnp.int32, (part, channels), 0) == part - 1
    is_left = (lax.broadcasted_iota(jnp.int32, (16, LANES), 0) & 2) == 0

    def activate(slot):
        block = lax.rem(w + slots[slot], nw)
        place = slice(slot * part, (slot + 1) * part)
        left_from = jnp.where(t == 0, jnp.maximum(block - 1, 0), block)
        right_from = jnp.where(t == nt - 1, jnp.minimum(block + 1, nw - 1), block)
        left_end = jnp.logical_and(t == 0, block == 0)
        right_end = jnp.logical_and(t == nt - 1, block == nw - 1)

        def step(frame, carry):
            edge = jnp.where(
                is_left, plane_one[frame * nw + left_from, 8:24, :], plane_one[frame * nw + right_from, 8:24, :]
            )
            edge = silu((edge - norm_edge[0]) * norm_edge[1] + norm_edge[2])
            for r in range(2):
                raw = blocks[frame * nw + block, r].astype(jnp.float32)
                middle = silu((raw - norm[0:1, :]) * norm[1:2, :] + norm[2:3, :])
                left = jnp.concatenate([edge[4 * k + r : 4 * k + r + 1] for k in range(blocks_of)], axis=1)
                right = jnp.concatenate([edge[4 * k + 2 + r : 4 * k + 3 + r] for k in range(blocks_of)], axis=1)
                left = jnp.where(left_end, middle[0:1, :], left)
                right = jnp.where(right_end, middle[part - 1 : part, :], right)
                before = jnp.where(first, left, pltpu.roll(middle, 1, 0)).astype(jnp.bfloat16)
                after = jnp.where(last, right, pltpu.roll(middle, part - 1, 0)).astype(jnp.bfloat16)
                middle = middle.astype(jnp.bfloat16)

                def put(moment, before=before, middle=middle, after=after, r=r):
                    acts[r, moment, place, 0:channels] = before
                    acts[r, moment, place, channels : 2 * channels] = middle
                    acts[r, moment, place, 2 * channels : 3 * channels] = after

                put(frame + 2)

                @pl.when(frame == 0)
                def _(put=put):
                    put(0)
                    put(1)

            return carry

        lax.fori_loop(0, nt, step, 0)

    def rim(side, stage, low, high):
        count = high - low
        window = acts[side, 2 : 2 + nt, low:high, :].reshape(nt * count, depth)
        early = jnp.dot(window, rim_pair[side], preferred_element_type=jnp.float32)
        late = jnp.dot(window, rim_last[side], preferred_element_type=jnp.float32)
        first_tap = early[:, 0:LANES].reshape(nt, count, LANES)
        second_tap = early[:, LANES:].reshape(nt, count, LANES)
        third_tap = late.reshape(nt, count, LANES)
        for frame in range(nt):
            total = first_tap[max(frame - 2, 0)] + second_tap[max(frame - 1, 0)] + third_tap[frame]
            rim_out[side, frame, low:high, :] = total.astype(jnp.bfloat16)
        at_end = h == jnp.where(side == 0, 0, nh - 1)

        @pl.when(at_end)
        def _():
            rim_in[side, :, low:high, :] = rim_out[side, :, low:high, :]

        @pl.when(jnp.logical_not(at_end))
        def _():
            pltpu.make_async_remote_copy(
                src_ref=rim_out.at[side, :, low:high, :], dst_ref=rim_in.at[1 - side, :, low:high, :],
                send_sem=rim_send.at[side, stage], recv_sem=rim_recv.at[1 - side, stage],
                device_id=(t, h - 1 + 2 * side, w), device_id_type=MESH,
            ).start()

    across = lax.rem(h, 2)
    for stage, (low, high) in enumerate(((0, near), (near, nw))):
        if stage == 0:
            all_arrived(blocks.at[pl.ds(0, nt * near - 1)], 1)
            own_block.wait()
        else:
            all_arrived(blocks.at[pl.ds(0, nt * (nw - near))], 2)
        for slot in range(low, high):
            activate(slot)
        rim(across, stage, low * part, high * part)
        rim(1 - across, stage, low * part, high * part)

    acc[...] = jnp.zeros((rows, 2 * LANES), jnp.float32)

    def pair_step(k, carry):
        acc[...] += jnp.dot(
            acts[0, pl.ds(k, nt)].reshape(rows, depth), pair_a[k], preferred_element_type=jnp.float32
        ) + jnp.dot(acts[1, pl.ds(k, nt)].reshape(rows, depth), pair_b[k], preferred_element_type=jnp.float32)
        return carry

    lax.fori_loop(0, 3, pair_step, 0)

    for side in range(2):
        at_end = (h == 0) if side == 0 else (h == nh - 1)

        @pl.when(jnp.logical_not(at_end))
        def _(side=side):
            for stage, (low, high) in enumerate(((0, near * part), (near * part, span))):
                into = rim_in.at[side, :, low:high, :]
                outof = rim_out.at[side, :, low:high, :]
                pltpu.make_async_copy(into, into, rim_recv.at[side, stage]).wait()
                pltpu.make_async_copy(outof, outof, rim_send.at[side, stage]).wait()

    sums = jnp.zeros((1, LANES), jnp.float32)
    for r in range(2):
        total = acc[:, r * LANES : (r + 1) * LANES] + rim_in[r].reshape(rows, LANES).astype(jnp.float32)
        conv[r] = total
        conv_out[r] = total.astype(jnp.bfloat16).reshape(nt, span, LANES)
        sums = sums + jnp.sum(total, axis=0, keepdims=True)
    mean = sums / (2 * rows)
    deviation = jnp.zeros((1, LANES), jnp.float32)
    for r in range(2):
        centered = conv[r] - mean
        deviation = deviation + jnp.sum(centered * centered, axis=0, keepdims=True)
    line_two[h] = jnp.zeros((8, LANES), jnp.float32)
    line_two[h, 0:1, :] = mean
    line_two[h, 1:2, :] = deviation
    line_loop(lambda j: remote(line_two.at[h], line_two.at[h], 4, (t, j, w)).start())

    own_place = back.at[:, pl.ds(t * part, part), pl.ds(pl.multiple_of(w * LANES, LANES), LANES)]
    for offset in far_first:
        y, q = plane_peer(offset)
        slot = slots.index(offset[1])
        remote(conv_out.at[:, y, slot * part : (slot + 1) * part, :], own_place, 5, (y, h, q)).start()
    own_back = pltpu.make_async_copy(conv_out.at[:, t, 0:part, :], own_place, local_sem.at[0])
    own_back.start()

    all_arrived(line_two.at[pl.ds(0, nh - 1)], 4)
    mean, deviation = combined(line_two[:, 0:1, :], line_two[:, 1:2, :], float(2 * rows), 0)
    plane_two[me] = jnp.zeros((8, LANES), jnp.float32)
    plane_two[me, 0:1, :] = mean
    plane_two[me, 1:2, :] = deviation
    for offset in far_first:
        y, q = plane_peer(offset)
        remote(plane_two.at[me], plane_two.at[me], 6, (y, h, q)).start()
    all_sent(plane_one.at[others], 0)
    all_sent(blocks.at[pl.ds(0, nt * near - 1)], 1)
    all_sent(blocks.at[pl.ds(0, nt * (nw - near))], 2)
    all_sent(line_one.at[pl.ds(0, nh - 1)], 3)
    all_sent(line_two.at[pl.ds(0, nh - 1)], 4)
    all_sent(blocks.at[others, :, :, 0:LANES], 5)
    all_arrived(blocks.at[others, :, :, 0:LANES], 5)
    own_back.wait()
    all_arrived(plane_two.at[others], 6)
    gathered = plane_two[...].reshape(nt, nw, 8, LANES)
    mean, deviation = combined(gathered[:, :, 0, :], gathered[:, :, 1, :], float(2 * rows * nh), 0)
    mean, inverse = group_norm_terms(mean, deviation, float(everywhere), float(width))
    norm[0:1, :] = jnp.concatenate(lane_blocks(mean), axis=1)
    norm[1:2, :] = jnp.concatenate(lane_blocks(inverse), axis=1) * gain_two[...]
    norm[2:3, :] = shift_two[...]
    for r in range(2):
        out[0, r] = silu(
            (back[r].astype(jnp.float32) - norm[0:1, :]) * norm[1:2, :] + norm[2:3, :]
        ).astype(jnp.bfloat16)
    all_sent(plane_two.at[others], 6)


def solution(mesh):
    nt, nh, nw = mesh.shape["tm"], mesh.shape["ha"], mesh.shape["wa"]

    def per_device(features, gain_one, shift_one, conv_weight, gain_two, shift_two):
        columns, channels = features.shape[2], features.shape[3]
        own = conv_weight.shape[4]
        plane, part, depth = nt * nw, columns // nt, 3 * channels
        span = nw * part
        rows = nt * span
        vmem = pl.BlockSpec(memory_space=pltpu.VMEM)
        bf16, f32 = jnp.bfloat16, jnp.float32
        return pl.pallas_call(
            functools.partial(kernel, nt, nh, nw),
            out_shape=pltpu.VMEM(features.shape, bf16),
            in_specs=[pl.BlockSpec(memory_space=pltpu.HBM)] * 6,
            out_specs=vmem,
            scratch_shapes=[
                pltpu.VMEM(features.shape, bf16),
                pltpu.VMEM((1, channels), f32),
                pltpu.VMEM((1, channels), f32),
                pltpu.VMEM((1, channels), f32),
                pltpu.VMEM((1, channels), f32),
                pltpu.VMEM((nt, 24, LANES), f32),
                pltpu.VMEM((plane, 2, part, channels), bf16),
                pltpu.VMEM((2, nt + 2, span, depth), bf16),
                pltpu.VMEM((3, depth, 2 * own), bf16),
                pltpu.VMEM((3, depth, 2 * own), bf16),
                pltpu.VMEM((2, depth, 2 * own), bf16),
                pltpu.VMEM((2, depth, own), bf16),
                pltpu.VMEM((rows, 2 * own), f32),
                pltpu.VMEM((2, rows, own), f32),
                pltpu.VMEM((2, nt, span, own), bf16),
                pltpu.VMEM((2, nt, span, own), bf16),
                pltpu.VMEM((2, nt, span, own), bf16),
                pltpu.VMEM((2, columns, channels), bf16),
                pltpu.VMEM((plane, 24, LANES), f32),
                pltpu.VMEM((nh, 8, LANES), f32),
                pltpu.VMEM((nh, 8, LANES), f32),
                pltpu.VMEM((plane, 8, LANES), f32),
                pltpu.VMEM((8, channels), f32),
                pltpu.VMEM((3, 16, LANES), f32),
                pltpu.SemaphoreType.DMA((5,)),
                pltpu.SemaphoreType.DMA((18,)),
                pltpu.SemaphoreType.DMA((1,)),
                pltpu.SemaphoreType.DMA((7,)),
                pltpu.SemaphoreType.DMA((7,)),
                pltpu.SemaphoreType.DMA((2, 2)),
                pltpu.SemaphoreType.DMA((2, 2)),
            ],
            compiler_params=pltpu.CompilerParams(
                collective_id=0, has_side_effects=True, vmem_limit_bytes=60 * 1024 * 1024
            ),
        )(
            features,
            gain_one.reshape(1, channels),
            shift_one.reshape(1, channels),
            conv_weight.reshape(3, 3, depth, own),
            gain_two.reshape(1, channels),
            shift_two.reshape(1, channels),
        )

    in_specs = (P("tm", "ha", "wa", None), P(), P(), P(None, None, None, None, "wa"), P(), P())
    return jax.shard_map(
        per_device, mesh=mesh, in_specs=in_specs, out_specs=P("tm", "ha", "wa", None), check_vma=False
    )
```

```python
import functools

import jax
import jax.numpy as jnp
from jax import lax
from jax.experimental import pallas as pl
from jax.experimental.pallas import tpu as pltpu
from jax.sharding import PartitionSpec as P

GROUPS = 32
LANES = 128
EPS = 1e-06
MESH = pl.DeviceIdType.MESH


def lane_blocks(rows):
    return [rows[k : k + 1, :] for k in range(rows.shape[0])]


def group_sum(values, width):
    axis = values.ndim - 1
    lane = lax.broadcasted_iota(jnp.int32, values.shape, axis)
    step = 1
    while step < width:
        ahead = pltpu.roll(values, step, axis)
        behind = pltpu.roll(values, LANES - step, axis)
        values = values + jnp.where((lane & step) != 0, ahead, behind)
        step *= 2
    return values


def combined(means, deviations, count, axis):
    mean = jnp.mean(means, axis=axis, keepdims=True)
    spread = means - mean
    total = jnp.sum(deviations, axis=axis) + count * jnp.sum(spread * spread, axis=axis)
    return jnp.squeeze(mean, axis), total


def group_norm_terms(mean, deviation, count, width):
    group_mean = group_sum(mean, width) / width
    spread = mean - group_mean
    group_var = group_sum(deviation + count * (spread * spread), width) / (count * width)
    return group_mean, lax.rsqrt(group_var + EPS)


def silu(v):
    half = 0.5 * v
    return half + half * jnp.tanh(half)


def hops(distance, count):
    return min(distance, count - distance)


def kernel(
    nt, nh, nw,
    feat_hbm, gain_one_hbm, shift_one_hbm, weight, gain_two_hbm, shift_two_hbm, out,
    feat, gain_one, shift_one, gain_two, shift_two,
    message, blocks, acts, pairs, rim_pair, rim_last, acc, conv, conv_out, rim_out, rim_in, back,
    plane_one, line_one, line_two, plane_two, norm, norm_edge,
    input_sem, weight_sem, local_sem, send_sem, recv_sem, rim_send, rim_recv,
):
    t, h, w = lax.axis_index("tm"), lax.axis_index("ha"), lax.axis_index("wa")
    plane = nt * nw
    me = t * nw + w
    columns, channels = feat.shape[2], feat.shape[3]
    part = columns // nt
    blocks_of = channels // LANES
    width = channels // GROUPS
    depth = 3 * channels
    span = nw * part
    rows = nt * span
    entries = 2 * columns
    everywhere = entries * plane * nh
    across = lax.rem(h, 2)
    offsets = [(a, b) for a in range(nt) for b in range(nw) if a or b]
    far_first = sorted(offsets, key=lambda d: -hops(d[0], nt) - hops(d[1], nw))

    def plane_peer(offset):
        return lax.rem(t + offset[0], nt), lax.rem(w + offset[1], nw)

    def line_loop(body):
        def step(i, carry):
            away = lax.div(i + 1, 2)
            offset = nh // 2 + jnp.where(lax.rem(i, 2) == 1, away, -away)
            body(lax.rem(h + offset, nh))
            return carry

        lax.fori_loop(0, nh - 1, step, 0)

    copy_in = [
        pltpu.make_async_copy(source, target, input_sem.at[n])
        for n, (source, target) in enumerate(
            (
                (feat_hbm, feat),
                (gain_one_hbm, gain_one),
                (shift_one_hbm, shift_one),
                (gain_two_hbm, gain_two),
                (shift_two_hbm, shift_two),
            )
        )
    ]
    copy_in[0].start()

    barrier = pltpu.get_barrier_semaphore()

    def greet(device):
        pl.semaphore_signal(barrier, inc=1, device_id=device, device_id_type=MESH)

    line_loop(lambda j: greet((t, j, w)))
    for offset in far_first:
        y, q = plane_peer(offset)
        greet((y, h, q))

    for copy in copy_in[1:]:
        copy.start()
    above = jnp.where(h == 0, 0, 2)
    below = jnp.where(h == nh - 1, 2, 0)
    left_half, right_half = pl.ds(0, LANES), pl.ds(LANES, LANES)
    weight_copies = []
    for side, row in ((0, above), (1, below)):
        weight_copies += [
            (weight.at[0, row], rim_pair.at[side, :, left_half]),
            (weight.at[1, row], rim_pair.at[side, :, right_half]),
            (weight.at[2, row], rim_last.at[side]),
        ]
    for k in range(3):
        weight_copies += [
            (weight.at[k, 1], pairs.at[0, k, :, left_half]),
            (weight.at[k, 0], pairs.at[0, k, :, right_half]),
            (weight.at[k, 2], pairs.at[1, k, :, left_half]),
            (weight.at[k, 1], pairs.at[1, k, :, right_half]),
        ]
    weight_copies = [
        pltpu.make_async_copy(source, target, weight_sem.at[n])
        for n, (source, target) in enumerate(weight_copies)
    ]

    copy_in[0].wait()
    for copy in weight_copies:
        copy.start()
    values = feat[0].astype(jnp.float32)
    flat = values.reshape(entries, channels)
    mean = jnp.mean(flat, axis=0, keepdims=True)
    centered = flat - mean
    deviation = jnp.sum(centered * centered, axis=0, keepdims=True)
    pieces = [mean[:, k * LANES : (k + 1) * LANES] for k in range(blocks_of)]
    pieces += [jnp.zeros((1, LANES), jnp.float32)] * (4 - blocks_of)
    pieces += [deviation[:, k * LANES : (k + 1) * LANES] for k in range(blocks_of)]
    pieces += [jnp.zeros((1, LANES), jnp.float32)] * (4 - blocks_of)
    local_terms = jnp.concatenate(pieces, axis=0)
    for y in range(nt):
        left = (y * part - 1) % columns
        right = (y * part + part) % columns
        four = jnp.concatenate(
            [values[r, c : c + 1, :] for c in (left, right) for r in range(2)], axis=0
        )
        pieces = [four[:, k * LANES : (k + 1) * LANES] for k in range(blocks_of)]
        pieces += [jnp.zeros((4, LANES), jnp.float32)] * (4 - blocks_of)
        message[y, 8:24, :] = jnp.concatenate(pieces, axis=0)
    line_one[h] = local_terms

    own_block = pltpu.make_async_copy(feat.at[0, :, pl.ds(t * part, part), :], blocks.at[me], local_sem.at[0])
    own_block.start()

    pl.semaphore_wait(barrier, plane - 1 + nh - 1)

    def remote(source, target, index, device):
        return pltpu.make_async_remote_copy(
            src_ref=source, dst_ref=target, send_sem=send_sem.at[index], recv_sem=recv_sem.at[index],
            device_id=device, device_id_type=MESH,
        )

    def all_arrived(buffer, index):
        pltpu.make_async_copy(buffer, buffer, recv_sem.at[index]).wait()

    def all_sent(buffer, index):
        pltpu.make_async_copy(buffer, buffer, send_sem.at[index]).wait()

    def send_row(r, stage):
        for offset in far_first:
            y, q = plane_peer(offset)
            remote(feat.at[0, r, pl.ds(y * part, part), :], blocks.at[me, r], 1 + stage, (y, h, q)).start()

    line_loop(lambda j: remote(line_one.at[h], line_one.at[h], 3, (t, j, w)).start())
    send_row(across, 0)
    others = pl.ds(0, plane - 1)
    all_arrived(line_one.at[pl.ds(0, nh - 1)], 3)
    mean, deviation = combined(line_one[:, 0:4, :], line_one[:, 4:8, :], float(entries), 0)
    combined_terms = jnp.concatenate([mean, deviation], axis=0)
    for y in range(nt):
        message[y, 0:8, :] = combined_terms
    for offset in far_first:
        y, q = plane_peer(offset)
        remote(message.at[y], plane_one.at[me], 0, (y, h, q)).start()
    send_row(1 - across, 1)
    plane_one[me] = message[t]
    for copy in copy_in[1:]:
        copy.wait()
    for copy in weight_copies:
        copy.wait()
    all_arrived(plane_one.at[others], 0)
    mean, deviation = combined(plane_one[:, 0:4, :], plane_one[:, 4:8, :], float(entries * nh), 0)
    mean, inverse = group_norm_terms(mean, deviation, float(everywhere), float(width))
    wide_mean = jnp.concatenate(lane_blocks(mean[0:blocks_of]), axis=1)
    wide_scale = jnp.concatenate(lane_blocks(inverse[0:blocks_of]), axis=1) * gain_one[...]
    norm[0:1, :] = wide_mean
    norm[1:2, :] = wide_scale
    norm[2:3, :] = shift_one[...]
    for n, vector in enumerate((wide_mean, wide_scale, shift_one[...])):
        for k in range(blocks_of):
            norm_edge[n, 4 * k : 4 * k + 4, :] = jnp.broadcast_to(
                vector[:, k * LANES : (k + 1) * LANES], (4, LANES)
            )
        if blocks_of < 4:
            norm_edge[n, 4 * blocks_of :, :] = jnp.zeros((16 - 4 * blocks_of, LANES), jnp.float32)

    first = lax.broadcasted_iota(jnp.int32, (part, channels), 0) == 0
    last = lax.broadcasted_iota(jnp.int32, (part, channels), 0) == part - 1
    is_left = (lax.broadcasted_iota(jnp.int32, (16, LANES), 0) & 2) == 0

    def activate(r):
        def step(pair, carry):
            for j in (2 * pair, 2 * pair + 1):
                frame, block = lax.div(j, nw), lax.rem(j, nw)
                left_from = jnp.where(t == 0, jnp.maximum(block - 1, 0), block)
                right_from = jnp.where(t == nt - 1, jnp.minimum(block + 1, nw - 1), block)
                left_end = jnp.logical_and(t == 0, block == 0)
                right_end = jnp.logical_and(t == nt - 1, block == nw - 1)
                edge = jnp.where(
                    is_left, plane_one[frame * nw + left_from, 8:24, :], plane_one[frame * nw + right_from, 8:24, :]
                )
                edge = silu((edge - norm_edge[0]) * norm_edge[1] + norm_edge[2])
                raw = blocks[j, r].astype(jnp.float32)
                middle = silu((raw - norm[0:1, :]) * norm[1:2, :] + norm[2:3, :])
                sides = [
                    jnp.where(r == 0, edge[4 * k : 4 * k + 3], edge[4 * k + 1 : 4 * k + 4]) for k in range(blocks_of)
                ]
                left = jnp.concatenate([piece[0:1] for piece in sides], axis=1)
                right = jnp.concatenate([piece[2:3] for piece in sides], axis=1)
                left = jnp.where(left_end, middle[0:1, :], left)
                right = jnp.where(right_end, middle[part - 1 : part, :], right)
                before = jnp.where(first, left, pltpu.roll(middle, 1, 0))
                after = jnp.where(last, right, pltpu.roll(middle, part - 1, 0))
                place = pl.ds(pl.multiple_of(block * part, part), part)
                acts[r, frame + 2, place, 0:channels] = before.astype(jnp.bfloat16)
                acts[r, frame + 2, place, channels : 2 * channels] = middle.astype(jnp.bfloat16)
                acts[r, frame + 2, place, 2 * channels : 3 * channels] = after.astype(jnp.bfloat16)
            return carry

        lax.fori_loop(0, plane // 2, step, 0)
        initial = acts[r, 2]
        acts[r, 0] = initial
        acts[r, 1] = initial

    def rim(side):
        window = acts[side, 2 : 2 + nt].reshape(rows, depth)
        early = jnp.dot(window, rim_pair[side], preferred_element_type=jnp.float32)
        late = jnp.dot(window, rim_last[side], preferred_element_type=jnp.float32)
        first_tap = early[:, 0:LANES].reshape(nt, span, LANES)
        second_tap = early[:, LANES:].reshape(nt, span, LANES)
        third_tap = late.reshape(nt, span, LANES)
        for frame in range(nt):
            total = first_tap[max(frame - 2, 0)] + second_tap[max(frame - 1, 0)] + third_tap[frame]
            rim_out[side, frame] = total.astype(jnp.bfloat16)
        at_end = h == jnp.where(side == 0, 0, nh - 1)

        @pl.when(at_end)
        def _():
            rim_in[side] = rim_out[side]

        @pl.when(jnp.logical_not(at_end))
        def _():
            pltpu.make_async_remote_copy(
                src_ref=rim_out.at[side], dst_ref=rim_in.at[1 - side],
                send_sem=rim_send.at[side], recv_sem=rim_recv.at[1 - side],
                device_id=(t, h - 1 + 2 * side, w), device_id_type=MESH,
            ).start()

    acc[...] = jnp.zeros((rows, 2 * LANES), jnp.float32)
    for stage in range(2):
        r = across if stage == 0 else 1 - across
        all_arrived(blocks.at[others, 0], 1 + stage)
        if stage == 0:
            own_block.wait()
        activate(r)
        rim(r)

        def pair_step(k, carry, r=r):
            acc[...] += jnp.dot(
                acts[r, pl.ds(k, nt)].reshape(rows, depth), pairs[r, k], preferred_element_type=jnp.float32
            )
            return carry

        lax.fori_loop(0, 3, pair_step, 0)

    for side in range(2):
        at_end = (h == 0) if side == 0 else (h == nh - 1)

        @pl.when(jnp.logical_not(at_end))
        def _(side=side):
            pltpu.make_async_copy(rim_in.at[side], rim_in.at[side], rim_recv.at[side]).wait()
            pltpu.make_async_copy(rim_out.at[side], rim_out.at[side], rim_send.at[side]).wait()

    sums = jnp.zeros((1, LANES), jnp.float32)
    for r in range(2):
        total = acc[:, r * LANES : (r + 1) * LANES] + rim_in[r].reshape(rows, LANES).astype(jnp.float32)
        conv[r] = total
        conv_out[r] = total.astype(jnp.bfloat16).reshape(nt, span, LANES)
        sums = sums + jnp.sum(total, axis=0, keepdims=True)
    mean = sums / (2 * rows)
    deviation = jnp.zeros((1, LANES), jnp.float32)
    for r in range(2):
        centered = conv[r] - mean
        deviation = deviation + jnp.sum(centered * centered, axis=0, keepdims=True)
    line_two[h] = jnp.zeros((8, LANES), jnp.float32)
    line_two[h, 0:1, :] = mean
    line_two[h, 1:2, :] = deviation
    line_loop(lambda j: remote(line_two.at[h], line_two.at[h], 4, (t, j, w)).start())

    def result_of(frame, block):
        return conv_out.at[:, frame, pl.ds(pl.multiple_of(block * part, part), part), :]

    own_place = back.at[:, pl.ds(t * part, part), pl.ds(pl.multiple_of(w * LANES, LANES), LANES)]
    for offset in far_first:
        y, q = plane_peer(offset)
        remote(result_of(y, q), own_place, 5, (y, h, q)).start()
    own_back = pltpu.make_async_copy(result_of(t, w), own_place, local_sem.at[0])
    own_back.start()

    all_arrived(line_two.at[pl.ds(0, nh - 1)], 4)
    mean, deviation = combined(line_two[:, 0:1, :], line_two[:, 1:2, :], float(2 * rows), 0)
    plane_two[me] = jnp.zeros((8, LANES), jnp.float32)
    plane_two[me, 0:1, :] = mean
    plane_two[me, 1:2, :] = deviation
    for offset in far_first:
        y, q = plane_peer(offset)
        remote(plane_two.at[me], plane_two.at[me], 6, (y, h, q)).start()
    all_sent(plane_one.at[others], 0)
    all_sent(blocks.at[others, 0], 1)
    all_sent(blocks.at[others, 0], 2)
    all_sent(line_one.at[pl.ds(0, nh - 1)], 3)
    all_sent(line_two.at[pl.ds(0, nh - 1)], 4)
    all_sent(blocks.at[others, :, :, 0:LANES], 5)
    all_arrived(blocks.at[others, :, :, 0:LANES], 5)
    own_back.wait()
    all_arrived(plane_two.at[others], 6)
    gathered = plane_two[...].reshape(nt, nw, 8, LANES)
    mean, deviation = combined(gathered[:, :, 0, :], gathered[:, :, 1, :], float(2 * rows * nh), 0)
    mean, inverse = group_norm_terms(mean, deviation, float(everywhere), float(width))
    norm[0:1, :] = jnp.concatenate(lane_blocks(mean), axis=1)
    norm[1:2, :] = jnp.concatenate(lane_blocks(inverse), axis=1) * gain_two[...]
    norm[2:3, :] = shift_two[...]
    for r in range(2):
        out[0, r] = silu(
            (back[r].astype(jnp.float32) - norm[0:1, :]) * norm[1:2, :] + norm[2:3, :]
        ).astype(jnp.bfloat16)
    all_sent(plane_two.at[others], 6)


def solution(mesh):
    nt, nh, nw = mesh.shape["tm"], mesh.shape["ha"], mesh.shape["wa"]

    def per_device(features, gain_one, shift_one, conv_weight, gain_two, shift_two):
        columns, channels = features.shape[2], features.shape[3]
        own = conv_weight.shape[4]
        plane, part, depth = nt * nw, columns // nt, 3 * channels
        span = nw * part
        rows = nt * span
        vmem = pl.BlockSpec(memory_space=pltpu.VMEM)
        bf16, f32 = jnp.bfloat16, jnp.float32
        return pl.pallas_call(
            functools.partial(kernel, nt, nh, nw),
            out_shape=pltpu.VMEM(features.shape, bf16),
            in_specs=[pl.BlockSpec(memory_space=pltpu.HBM)] * 6,
            out_specs=vmem,
            scratch_shapes=[
                pltpu.VMEM(features.shape, bf16),
                pltpu.VMEM((1, channels), f32),
                pltpu.VMEM((1, channels), f32),
                pltpu.VMEM((1, channels), f32),
                pltpu.VMEM((1, channels), f32),
                pltpu.VMEM((nt, 24, LANES), f32),
                pltpu.VMEM((plane, 2, part, channels), bf16),
                pltpu.VMEM((2, nt + 2, span, depth), bf16),
                pltpu.VMEM((2, 3, depth, 2 * own), bf16),
                pltpu.VMEM((2, depth, 2 * own), bf16),
                pltpu.VMEM((2, depth, own), bf16),
                pltpu.VMEM((rows, 2 * own), f32),
                pltpu.VMEM((2, rows, own), f32),
                pltpu.VMEM((2, nt, span, own), bf16),
                pltpu.VMEM((2, nt, span, own), bf16),
                pltpu.VMEM((2, nt, span, own), bf16),
                pltpu.VMEM((2, columns, channels), bf16),
                pltpu.VMEM((plane, 24, LANES), f32),
                pltpu.VMEM((nh, 8, LANES), f32),
                pltpu.VMEM((nh, 8, LANES), f32),
                pltpu.VMEM((plane, 8, LANES), f32),
                pltpu.VMEM((8, channels), f32),
                pltpu.VMEM((3, 16, LANES), f32),
                pltpu.SemaphoreType.DMA((5,)),
                pltpu.SemaphoreType.DMA((18,)),
                pltpu.SemaphoreType.DMA((1,)),
                pltpu.SemaphoreType.DMA((7,)),
                pltpu.SemaphoreType.DMA((7,)),
                pltpu.SemaphoreType.DMA((2,)),
                pltpu.SemaphoreType.DMA((2,)),
            ],
            compiler_params=pltpu.CompilerParams(
                collective_id=0, has_side_effects=True, vmem_limit_bytes=60 * 1024 * 1024
            ),
        )(
            features,
            gain_one.reshape(1, channels),
            shift_one.reshape(1, channels),
            conv_weight.reshape(3, 3, depth, own),
            gain_two.reshape(1, channels),
            shift_two.reshape(1, channels),
        )

    in_specs = (P("tm", "ha", "wa", None), P(), P(), P(None, None, None, None, "wa"), P(), P())
    return jax.shard_map(
        per_device, mesh=mesh, in_specs=in_specs, out_specs=P("tm", "ha", "wa", None), check_vma=False
    )
```

```python
import functools

import jax
import jax.numpy as jnp
from jax import lax
from jax.experimental import pallas as pl
from jax.experimental.pallas import tpu as pltpu
from jax.sharding import PartitionSpec as P

GROUPS = 32
LANES = 128
EPS = 1e-06
MESH = pl.DeviceIdType.MESH


def lane_blocks(rows):
    return [rows[k : k + 1, :] for k in range(rows.shape[0])]


def group_sum(values, width):
    axis = values.ndim - 1
    lane = lax.broadcasted_iota(jnp.int32, values.shape, axis)
    step = 1
    while step < width:
        ahead = pltpu.roll(values, step, axis)
        behind = pltpu.roll(values, LANES - step, axis)
        values = values + jnp.where((lane & step) != 0, ahead, behind)
        step *= 2
    return values


def combined(means, deviations, count, axis):
    mean = jnp.mean(means, axis=axis, keepdims=True)
    spread = means - mean
    total = jnp.sum(deviations, axis=axis) + count * jnp.sum(spread * spread, axis=axis)
    return jnp.squeeze(mean, axis), total


def grouped_terms(mean, deviation, count, width):
    group_mean = group_sum(mean, width) / width
    spread = mean - group_mean
    return group_mean, group_sum(deviation + count * (spread * spread), width)


def group_norm_terms(mean, deviation, count, width):
    group_mean, group_deviation = grouped_terms(mean, deviation, count, width)
    return group_mean, lax.rsqrt(group_deviation / (count * width) + EPS)


def silu_of_double(half):
    return half + half * jnp.tanh(half)


def hops(distance, count):
    return min(distance, count - distance)


def kernel(
    nt, nh, nw,
    feat_hbm, gain_one_hbm, shift_one_hbm, weight, gain_two_hbm, shift_two_hbm, out,
    feat, gain_one, shift_one, gain_two, shift_two,
    edge_out, blocks, edges, acts, pairs, rim_pair, rim_last, acc, conv, conv_out, rim_out, rim_in, back,
    plane_one, line_one, line_two, plane_two, norm, norm_edge,
    input_sem, weight_sem, local_sem, send_sem, recv_sem, rim_send, rim_recv,
):
    t, h, w = lax.axis_index("tm"), lax.axis_index("ha"), lax.axis_index("wa")
    plane = nt * nw
    me = t * nw + w
    columns, channels = feat.shape[2], feat.shape[3]
    part = columns // nt
    blocks_of = channels // LANES
    width = channels // GROUPS
    depth = 3 * channels
    span = nw * part
    rows = nt * span
    entries = 2 * columns
    everywhere = entries * plane * nh
    across = lax.rem(h, 2)
    offsets = [(a, b) for a in range(nt) for b in range(nw) if a or b]
    far_first = sorted(offsets, key=lambda d: -hops(d[0], nt) - hops(d[1], nw))

    def plane_peer(offset):
        return lax.rem(t + offset[0], nt), lax.rem(w + offset[1], nw)

    def line_loop(body):
        def step(i, carry):
            away = lax.div(i + 1, 2)
            offset = nh // 2 + jnp.where(lax.rem(i, 2) == 1, away, -away)
            body(lax.rem(h + offset, nh))
            return carry

        lax.fori_loop(0, nh - 1, step, 0)

    copy_in = [
        pltpu.make_async_copy(source, target, input_sem.at[n])
        for n, (source, target) in enumerate(
            (
                (feat_hbm, feat),
                (gain_one_hbm, gain_one),
                (shift_one_hbm, shift_one),
                (gain_two_hbm, gain_two),
                (shift_two_hbm, shift_two),
            )
        )
    ]
    copy_in[0].start()

    barrier = pltpu.get_barrier_semaphore()

    def greet(device):
        pl.semaphore_signal(barrier, inc=1, device_id=device, device_id_type=MESH)

    line_loop(lambda j: greet((t, j, w)))
    for offset in far_first:
        y, q = plane_peer(offset)
        greet((y, h, q))

    for copy in copy_in[1:]:
        copy.start()
    above = jnp.where(h == 0, 0, 2)
    below = jnp.where(h == nh - 1, 2, 0)
    left_half, right_half = pl.ds(0, LANES), pl.ds(LANES, LANES)
    weight_copies = []
    for side, row in ((0, above), (1, below)):
        weight_copies += [
            (weight.at[0, row], rim_pair.at[side, :, left_half]),
            (weight.at[1, row], rim_pair.at[side, :, right_half]),
            (weight.at[2, row], rim_last.at[side]),
        ]
    for k in range(3):
        weight_copies += [
            (weight.at[k, 1], pairs.at[0, k, :, left_half]),
            (weight.at[k, 0], pairs.at[0, k, :, right_half]),
            (weight.at[k, 2], pairs.at[1, k, :, left_half]),
            (weight.at[k, 1], pairs.at[1, k, :, right_half]),
        ]
    weight_copies = [
        pltpu.make_async_copy(source, target, weight_sem.at[n])
        for n, (source, target) in enumerate(weight_copies)
    ]

    copy_in[0].wait()
    for copy in weight_copies:
        copy.start()
    values = feat[0].astype(jnp.float32)
    flat = values.reshape(entries, channels)
    mean = jnp.mean(flat, axis=0, keepdims=True)
    centered = flat - mean
    deviation = jnp.sum(centered * centered, axis=0, keepdims=True)
    pieces = [mean[:, k * LANES : (k + 1) * LANES] for k in range(blocks_of)]
    pieces += [jnp.zeros((1, LANES), jnp.float32)] * (4 - blocks_of)
    means = jnp.concatenate(pieces, axis=0)
    pieces = [deviation[:, k * LANES : (k + 1) * LANES] for k in range(blocks_of)]
    pieces += [jnp.zeros((1, LANES), jnp.float32)] * (4 - blocks_of)
    line_one[h] = jnp.concatenate(
        grouped_terms(means, jnp.concatenate(pieces, axis=0), float(entries), float(width)), axis=0
    )
    for y in range(nt):
        left = (y * part - 1) % columns
        right = (y * part + part) % columns
        four = jnp.concatenate(
            [values[r, c : c + 1, :] for c in (left, right) for r in range(2)], axis=0
        )
        pieces = [four[:, k * LANES : (k + 1) * LANES] for k in range(blocks_of)]
        pieces += [jnp.zeros((4, LANES), jnp.float32)] * (4 - blocks_of)
        edge_out[y] = jnp.concatenate(pieces, axis=0).astype(jnp.bfloat16)
    edges[me] = edge_out[t]

    own_block = pltpu.make_async_copy(feat.at[0, :, pl.ds(t * part, part), :], blocks.at[me], local_sem.at[0])
    own_block.start()

    pl.semaphore_wait(barrier, plane - 1 + nh - 1)

    def remote(source, target, index, device):
        return pltpu.make_async_remote_copy(
            src_ref=source, dst_ref=target, send_sem=send_sem.at[index], recv_sem=recv_sem.at[index],
            device_id=device, device_id_type=MESH,
        )

    def all_arrived(buffer, index):
        pltpu.make_async_copy(buffer, buffer, recv_sem.at[index]).wait()

    def all_sent(buffer, index):
        pltpu.make_async_copy(buffer, buffer, send_sem.at[index]).wait()

    def send_row(r, stage):
        for offset in far_first:
            y, q = plane_peer(offset)
            remote(feat.at[0, r, pl.ds(y * part, part), :], blocks.at[me, r], 1 + stage, (y, h, q)).start()

    line_loop(lambda j: remote(line_one.at[h], line_one.at[h], 3, (t, j, w)).start())
    send_row(across, 0)
    for offset in far_first:
        y, q = plane_peer(offset)
        remote(edge_out.at[y], edges.at[me], 7, (y, h, q)).start()
    others = pl.ds(0, plane - 1)
    all_arrived(line_one.at[pl.ds(0, nh - 1)], 3)
    mean, deviation = combined(line_one[:, 0:4, :], line_one[:, 4:8, :], float(entries * width), 0)
    plane_one[me] = jnp.concatenate([mean, deviation], axis=0)
    for offset in far_first:
        y, q = plane_peer(offset)
        remote(plane_one.at[me], plane_one.at[me], 0, (y, h, q)).start()
    send_row(1 - across, 1)
    for copy in copy_in[1:]:
        copy.wait()
    for copy in weight_copies:
        copy.wait()
    all_arrived(plane_one.at[others], 0)
    mean, deviation = combined(plane_one[:, 0:4, :], plane_one[:, 4:8, :], float(entries * width * nh), 0)
    inverse = lax.rsqrt(deviation / float(everywhere * width) + EPS)
    wide_mean = jnp.concatenate(lane_blocks(mean[0:blocks_of]), axis=1)
    wide_scale = jnp.concatenate(lane_blocks(inverse[0:blocks_of]), axis=1) * (0.5 * gain_one[...])
    wide_shift = 0.5 * shift_one[...]
    norm[0:1, :] = wide_mean
    norm[1:2, :] = wide_scale
    norm[2:3, :] = wide_shift
    for n, vector in enumerate((wide_mean, wide_scale, wide_shift)):
        for k in range(blocks_of):
            norm_edge[n, 4 * k : 4 * k + 4, :] = jnp.broadcast_to(
                vector[:, k * LANES : (k + 1) * LANES], (4, LANES)
            )
        if blocks_of < 4:
            norm_edge[n, 4 * blocks_of :, :] = jnp.zeros((16 - 4 * blocks_of, LANES), jnp.float32)

    sublane = lax.broadcasted_iota(jnp.int32, (8, channels), 0)
    first, last = sublane == 0, sublane == 7
    is_left = (lax.broadcasted_iota(jnp.int32, (16, LANES), 0) & 2) == 0

    def activate(r):
        def step(pair, carry):
            for j in (2 * pair, 2 * pair + 1):
                frame, block = lax.div(j, nw), lax.rem(j, nw)
                left_from = jnp.where(t == 0, jnp.maximum(block - 1, 0), block)
                right_from = jnp.where(t == nt - 1, jnp.minimum(block + 1, nw - 1), block)
                left_end = jnp.logical_and(t == 0, block == 0)
                right_end = jnp.logical_and(t == nt - 1, block == nw - 1)
                edge = jnp.where(
                    is_left,
                    edges[frame * nw + left_from].astype(jnp.float32),
                    edges[frame * nw + right_from].astype(jnp.float32),
                )
                edge = silu_of_double((edge - norm_edge[0]) * norm_edge[1] + norm_edge[2])
                raw = blocks[j, r].astype(jnp.float32)
                middle = silu_of_double((raw - norm[0:1, :]) * norm[1:2, :] + norm[2:3, :])
                sides = [
                    jnp.where(r == 0, edge[4 * k : 4 * k + 3], edge[4 * k + 1 : 4 * k + 4]) for k in range(blocks_of)
                ]
                left = jnp.concatenate([piece[0:1] for piece in sides], axis=1)
                right = jnp.concatenate([piece[2:3] for piece in sides], axis=1)
                left = jnp.where(left_end, middle[0:1, :], left)
                right = jnp.where(right_end, middle[part - 1 : part, :], right)
                before = pltpu.roll(middle, 1, 0)
                before = jnp.concatenate([jnp.where(first, left, before[0:8]), before[8:]], axis=0)
                after = pltpu.roll(middle, part - 1, 0)
                after = jnp.concatenate([after[: part - 8], jnp.where(last, right, after[part - 8 :])], axis=0)
                place = pl.ds(pl.multiple_of(block * part, part), part)
                acts[r, frame, place, 0:channels] = before.astype(jnp.bfloat16)
                acts[r, frame, place, channels : 2 * channels] = middle.astype(jnp.bfloat16)
                acts[r, frame, place, 2 * channels : 3 * channels] = after.astype(jnp.bfloat16)
            return carry

        lax.fori_loop(0, plane // 2, step, 0)

    def product(r, frames, taps):
        window = acts[r, 0:frames].reshape(frames * span, depth)
        return jnp.dot(window, taps, preferred_element_type=jnp.float32).reshape(frames, span, taps.shape[1])

    def rim(side):
        early = product(side, nt - 1, rim_pair[side])
        third_tap = product(side, nt, rim_last[side])
        first_tap, second_tap = early[:, :, 0:LANES], early[:, :, LANES:]
        for frame in range(nt):
            total = first_tap[max(frame - 2, 0)] + second_tap[max(frame - 1, 0)] + third_tap[frame]
            rim_out[side, frame] = total.astype(jnp.bfloat16)
        at_end = h == jnp.where(side == 0, 0, nh - 1)

        @pl.when(at_end)
        def _():
            rim_in[side] = rim_out[side]

        @pl.when(jnp.logical_not(at_end))
        def _():
            pltpu.make_async_remote_copy(
                src_ref=rim_out.at[side], dst_ref=rim_in.at[1 - side],
                send_sem=rim_send.at[side], recv_sem=rim_recv.at[1 - side],
                device_id=(t, h - 1 + 2 * side, w), device_id_type=MESH,
            ).start()

    for stage in range(2):
        r = across if stage == 0 else 1 - across
        all_arrived(blocks.at[others, 0], 1 + stage)
        if stage == 0:
            own_block.wait()
            all_arrived(edges.at[others], 7)
        activate(r)
        rim(r)

        for k in range(3):
            made = product(r, nt - 2 + k, pairs[r, k])
            for frame in range(nt):
                part_sum = made[max(frame - 2 + k, 0)]
                acc[frame] = part_sum if stage == 0 and k == 0 else acc[frame] + part_sum

    for side in range(2):
        at_end = (h == 0) if side == 0 else (h == nh - 1)

        @pl.when(jnp.logical_not(at_end))
        def _(side=side):
            pltpu.make_async_copy(rim_in.at[side], rim_in.at[side], rim_recv.at[side]).wait()
            pltpu.make_async_copy(rim_out.at[side], rim_out.at[side], rim_send.at[side]).wait()

    sums = jnp.zeros((1, LANES), jnp.float32)
    for r in range(2):
        total = acc[:, :, r * LANES : (r + 1) * LANES] + rim_in[r].astype(jnp.float32)
        conv[r] = total.reshape(rows, LANES)
        conv_out[r] = total.astype(jnp.bfloat16)
        sums = sums + jnp.sum(total.reshape(rows, LANES), axis=0, keepdims=True)
    mean = sums / (2 * rows)
    deviation = jnp.zeros((1, LANES), jnp.float32)
    for r in range(2):
        centered = conv[r] - mean
        deviation = deviation + jnp.sum(centered * centered, axis=0, keepdims=True)
    line_two[h] = jnp.zeros((8, LANES), jnp.float32)
    line_two[h, 0:1, :] = mean
    line_two[h, 1:2, :] = deviation
    line_loop(lambda j: remote(line_two.at[h], line_two.at[h], 4, (t, j, w)).start())

    def result_of(frame, block):
        return conv_out.at[:, frame, pl.ds(pl.multiple_of(block * part, part), part), :]

    own_place = back.at[:, pl.ds(t * part, part), pl.ds(pl.multiple_of(w * LANES, LANES), LANES)]
    for offset in far_first:
        y, q = plane_peer(offset)
        remote(result_of(y, q), own_place, 5, (y, h, q)).start()
    own_back = pltpu.make_async_copy(result_of(t, w), own_place, local_sem.at[0])
    own_back.start()

    all_arrived(line_two.at[pl.ds(0, nh - 1)], 4)
    mean, deviation = combined(line_two[:, 0:1, :], line_two[:, 1:2, :], float(2 * rows), 0)
    plane_two[me] = jnp.zeros((8, LANES), jnp.float32)
    plane_two[me, 0:1, :] = mean
    plane_two[me, 1:2, :] = deviation
    for offset in far_first:
        y, q = plane_peer(offset)
        remote(plane_two.at[me], plane_two.at[me], 6, (y, h, q)).start()
    all_sent(plane_one.at[others], 0)
    all_sent(edges.at[others], 7)
    all_sent(blocks.at[others, 0], 1)
    all_sent(blocks.at[others, 0], 2)
    all_sent(line_one.at[pl.ds(0, nh - 1)], 3)
    all_sent(line_two.at[pl.ds(0, nh - 1)], 4)
    all_sent(blocks.at[others, :, :, 0:LANES], 5)
    all_arrived(blocks.at[others, :, :, 0:LANES], 5)
    own_back.wait()
    all_arrived(plane_two.at[others], 6)
    gathered = plane_two[...].reshape(nt, nw, 8, LANES)
    mean, deviation = combined(gathered[:, :, 0, :], gathered[:, :, 1, :], float(2 * rows * nh), 0)
    mean, inverse = group_norm_terms(mean, deviation, float(everywhere), float(width))
    norm[0:1, :] = jnp.concatenate(lane_blocks(mean), axis=1)
    norm[1:2, :] = jnp.concatenate(lane_blocks(inverse), axis=1) * (0.5 * gain_two[...])
    norm[2:3, :] = 0.5 * shift_two[...]
    for r in range(2):
        out[0, r] = silu_of_double(
            (back[r].astype(jnp.float32) - norm[0:1, :]) * norm[1:2, :] + norm[2:3, :]
        ).astype(jnp.bfloat16)
    all_sent(plane_two.at[others], 6)


def solution(mesh):
    nt, nh, nw = mesh.shape["tm"], mesh.shape["ha"], mesh.shape["wa"]

    def per_device(features, gain_one, shift_one, conv_weight, gain_two, shift_two):
        columns, channels = features.shape[2], features.shape[3]
        own = conv_weight.shape[4]
        plane, part, depth = nt * nw, columns // nt, 3 * channels
        span = nw * part
        rows = nt * span
        vmem = pl.BlockSpec(memory_space=pltpu.VMEM)
        bf16, f32 = jnp.bfloat16, jnp.float32
        return pl.pallas_call(
            functools.partial(kernel, nt, nh, nw),
            out_shape=pltpu.VMEM(features.shape, bf16),
            in_specs=[pl.BlockSpec(memory_space=pltpu.HBM)] * 6,
            out_specs=vmem,
            scratch_shapes=[
                pltpu.VMEM(features.shape, bf16),
                pltpu.VMEM((1, channels), f32),
                pltpu.VMEM((1, channels), f32),
                pltpu.VMEM((1, channels), f32),
                pltpu.VMEM((1, channels), f32),
                pltpu.VMEM((nt, 16, LANES), bf16),
                pltpu.VMEM((plane, 2, part, channels), bf16),
                pltpu.VMEM((plane, 16, LANES), bf16),
                pltpu.VMEM((2, nt, span, depth), bf16),
                pltpu.VMEM((2, 3, depth, 2 * own), bf16),
                pltpu.VMEM((2, depth, 2 * own), bf16),
                pltpu.VMEM((2, depth, own), bf16),
                pltpu.VMEM((nt, span, 2 * own), f32),
                pltpu.VMEM((2, rows, own), f32),
                pltpu.VMEM((2, nt, span, own), bf16),
                pltpu.VMEM((2, nt, span, own), bf16),
                pltpu.VMEM((2, nt, span, own), bf16),
                pltpu.VMEM((2, columns, channels), bf16),
                pltpu.VMEM((plane, 8, LANES), f32),
                pltpu.VMEM((nh, 8, LANES), f32),
                pltpu.VMEM((nh, 8, LANES), f32),
                pltpu.VMEM((plane, 8, LANES), f32),
                pltpu.VMEM((8, channels), f32),
                pltpu.VMEM((3, 16, LANES), f32),
                pltpu.SemaphoreType.DMA((5,)),
                pltpu.SemaphoreType.DMA((18,)),
                pltpu.SemaphoreType.DMA((1,)),
                pltpu.SemaphoreType.DMA((8,)),
                pltpu.SemaphoreType.DMA((8,)),
                pltpu.SemaphoreType.DMA((2,)),
                pltpu.SemaphoreType.DMA((2,)),
            ],
            compiler_params=pltpu.CompilerParams(
                collective_id=0, has_side_effects=True, vmem_limit_bytes=60 * 1024 * 1024
            ),
        )(
            features,
            gain_one.reshape(1, channels),
            shift_one.reshape(1, channels),
            conv_weight.reshape(3, 3, depth, own),
            gain_two.reshape(1, channels),
            shift_two.reshape(1, channels),
        )

    in_specs = (P("tm", "ha", "wa", None), P(), P(), P(None, None, None, None, "wa"), P(), P())
    return jax.shard_map(
        per_device, mesh=mesh, in_specs=in_specs, out_specs=P("tm", "ha", "wa", None), check_vma=False
    )
```

```python
import functools

import jax
import jax.numpy as jnp
from jax import lax
from jax.experimental import pallas as pl
from jax.experimental.pallas import tpu as pltpu
from jax.sharding import PartitionSpec as P

GROUPS = 32
LANES = 128
EPS = 1e-06
MESH = pl.DeviceIdType.MESH


def lane_blocks(rows):
    return [rows[k : k + 1, :] for k in range(rows.shape[0])]


def group_sum(values, width):
    axis = values.ndim - 1
    lane = lax.broadcasted_iota(jnp.int32, values.shape, axis)
    step = 1
    while step < width:
        ahead = pltpu.roll(values, step, axis)
        behind = pltpu.roll(values, LANES - step, axis)
        values = values + jnp.where((lane & step) != 0, ahead, behind)
        step *= 2
    return values


def combined(means, deviations, count, axis):
    mean = jnp.mean(means, axis=axis, keepdims=True)
    spread = means - mean
    total = jnp.sum(deviations, axis=axis) + count * jnp.sum(spread * spread, axis=axis)
    return jnp.squeeze(mean, axis), total


def grouped_terms(mean, deviation, count, width):
    group_mean = group_sum(mean, width) / width
    spread = mean - group_mean
    return group_mean, group_sum(deviation + count * (spread * spread), width)


def silu_of_double(half):
    return half + half * jnp.tanh(half)


def hops(distance, count):
    return min(distance, count - distance)


def kernel(
    nt, nh, nw,
    feat_hbm, gain_one_hbm, shift_one_hbm, weight, gain_two_hbm, shift_two_hbm, back, mean_two, scale_two, half_shift,
    feat, gain_one, shift_one, gain_two, shift_two,
    edge_out, blocks, edges, acts, pairs, rim_pair, rim_last, acc, conv_out, rim_out, rim_in,
    plane_one, line_one, line_two, plane_two, norm, norm_edge,
    input_sem, weight_sem, local_sem, send_sem, recv_sem, rim_send, rim_recv,
):
    t, h, w = lax.axis_index("tm"), lax.axis_index("ha"), lax.axis_index("wa")
    plane = nt * nw
    me = t * nw + w
    columns, channels = feat.shape[2], feat.shape[3]
    part = columns // nt
    blocks_of = channels // LANES
    width = channels // GROUPS
    depth = 3 * channels
    span = nw * part
    rows = nt * span
    entries = 2 * columns
    everywhere = entries * plane * nh
    across = lax.rem(h, 2)
    offsets = [(a, b) for a in range(nt) for b in range(nw) if a or b]
    far_first = sorted(offsets, key=lambda d: -hops(d[0], nt) - hops(d[1], nw))

    def plane_peer(offset):
        return lax.rem(t + offset[0], nt), lax.rem(w + offset[1], nw)

    def line_loop(body):
        def step(i, carry):
            away = lax.div(i + 1, 2)
            offset = nh // 2 + jnp.where(lax.rem(i, 2) == 1, away, -away)
            body(lax.rem(h + offset, nh))
            return carry

        lax.fori_loop(0, nh - 1, step, 0)

    copy_in = [
        pltpu.make_async_copy(source, target, input_sem.at[n])
        for n, (source, target) in enumerate(
            (
                (feat_hbm, feat),
                (gain_one_hbm, gain_one),
                (shift_one_hbm, shift_one),
                (gain_two_hbm, gain_two),
                (shift_two_hbm, shift_two),
            )
        )
    ]
    copy_in[0].start()

    barrier = pltpu.get_barrier_semaphore()

    def greet(device):
        pl.semaphore_signal(barrier, inc=1, device_id=device, device_id_type=MESH)

    line_loop(lambda j: greet((t, j, w)))
    for offset in far_first:
        y, q = plane_peer(offset)
        greet((y, h, q))

    for copy in copy_in[1:]:
        copy.start()
    above = jnp.where(h == 0, 0, 2)
    below = jnp.where(h == nh - 1, 2, 0)
    left_half, right_half = pl.ds(0, LANES), pl.ds(LANES, LANES)
    weight_copies = []
    for side, row in ((0, above), (1, below)):
        weight_copies += [
            (weight.at[0, row], rim_pair.at[side, :, left_half]),
            (weight.at[1, row], rim_pair.at[side, :, right_half]),
            (weight.at[2, row], rim_last.at[side]),
        ]
    for k in range(3):
        weight_copies += [
            (weight.at[k, 1], pairs.at[0, k, :, left_half]),
            (weight.at[k, 0], pairs.at[0, k, :, right_half]),
            (weight.at[k, 2], pairs.at[1, k, :, left_half]),
            (weight.at[k, 1], pairs.at[1, k, :, right_half]),
        ]
    weight_copies = [
        pltpu.make_async_copy(source, target, weight_sem.at[n])
        for n, (source, target) in enumerate(weight_copies)
    ]

    copy_in[0].wait()
    for copy in weight_copies:
        copy.start()
    values = feat[0].astype(jnp.float32)
    flat = values.reshape(entries, channels)
    mean = jnp.mean(flat, axis=0, keepdims=True)
    centered = flat - mean
    deviation = jnp.sum(centered * centered, axis=0, keepdims=True)
    pieces = [mean[:, k * LANES : (k + 1) * LANES] for k in range(blocks_of)]
    pieces += [jnp.zeros((1, LANES), jnp.float32)] * (4 - blocks_of)
    means = jnp.concatenate(pieces, axis=0)
    pieces = [deviation[:, k * LANES : (k + 1) * LANES] for k in range(blocks_of)]
    pieces += [jnp.zeros((1, LANES), jnp.float32)] * (4 - blocks_of)
    line_one[h] = jnp.concatenate(
        grouped_terms(means, jnp.concatenate(pieces, axis=0), float(entries), float(width)), axis=0
    )
    for y in range(nt):
        left = (y * part - 1) % columns
        right = (y * part + part) % columns
        four = jnp.concatenate(
            [values[r, c : c + 1, :] for c in (left, right) for r in range(2)], axis=0
        )
        pieces = [four[:, k * LANES : (k + 1) * LANES] for k in range(blocks_of)]
        pieces += [jnp.zeros((4, LANES), jnp.float32)] * (4 - blocks_of)
        edge_out[y] = jnp.concatenate(pieces, axis=0).astype(jnp.bfloat16)
    edges[me] = edge_out[t]

    own_block = pltpu.make_async_copy(feat.at[0, :, pl.ds(t * part, part), :], blocks.at[me], local_sem.at[0])
    own_block.start()

    pl.semaphore_wait(barrier, plane - 1 + nh - 1)

    def remote(source, target, index, device):
        return pltpu.make_async_remote_copy(
            src_ref=source, dst_ref=target, send_sem=send_sem.at[index], recv_sem=recv_sem.at[index],
            device_id=device, device_id_type=MESH,
        )

    def all_arrived(buffer, index):
        pltpu.make_async_copy(buffer, buffer, recv_sem.at[index]).wait()

    def all_sent(buffer, index):
        pltpu.make_async_copy(buffer, buffer, send_sem.at[index]).wait()

    def send_row(r, stage):
        for offset in far_first:
            y, q = plane_peer(offset)
            remote(feat.at[0, r, pl.ds(y * part, part), :], blocks.at[me, r], 1 + stage, (y, h, q)).start()

    line_loop(lambda j: remote(line_one.at[h], line_one.at[h], 3, (t, j, w)).start())
    send_row(across, 0)
    for offset in far_first:
        y, q = plane_peer(offset)
        remote(edge_out.at[y], edges.at[me], 7, (y, h, q)).start()
    others = pl.ds(0, plane - 1)
    all_arrived(line_one.at[pl.ds(0, nh - 1)], 3)
    mean, deviation = combined(line_one[:, 0:4, :], line_one[:, 4:8, :], float(entries * width), 0)
    plane_one[me] = jnp.concatenate([mean, deviation], axis=0)
    for offset in far_first:
        y, q = plane_peer(offset)
        remote(plane_one.at[me], plane_one.at[me], 0, (y, h, q)).start()
    send_row(1 - across, 1)
    for copy in copy_in[1:]:
        copy.wait()
    for copy in weight_copies:
        copy.wait()
    all_arrived(plane_one.at[others], 0)
    mean, deviation = combined(plane_one[:, 0:4, :], plane_one[:, 4:8, :], float(entries * width * nh), 0)
    inverse = lax.rsqrt(deviation / float(everywhere * width) + EPS)
    wide_mean = jnp.concatenate(lane_blocks(mean[0:blocks_of]), axis=1)
    wide_scale = jnp.concatenate(lane_blocks(inverse[0:blocks_of]), axis=1) * (0.5 * gain_one[...])
    wide_shift = 0.5 * shift_one[...]
    norm[0:1, :] = wide_mean
    norm[1:2, :] = wide_scale
    norm[2:3, :] = wide_shift
    for n, vector in enumerate((wide_mean, wide_scale, wide_shift)):
        for k in range(blocks_of):
            norm_edge[n, 4 * k : 4 * k + 4, :] = jnp.broadcast_to(
                vector[:, k * LANES : (k + 1) * LANES], (4, LANES)
            )
        if blocks_of < 4:
            norm_edge[n, 4 * blocks_of :, :] = jnp.zeros((16 - 4 * blocks_of, LANES), jnp.float32)

    sublane = lax.broadcasted_iota(jnp.int32, (8, channels), 0)
    first, last = sublane == 0, sublane == 7
    is_left = (lax.broadcasted_iota(jnp.int32, (16, LANES), 0) & 2) == 0

    def activate(r):
        def step(pair, carry):
            for j in (4 * pair, 4 * pair + 1, 4 * pair + 2, 4 * pair + 3):
                frame, block = lax.div(j, nw), lax.rem(j, nw)
                left_from = jnp.where(t == 0, jnp.maximum(block - 1, 0), block)
                right_from = jnp.where(t == nt - 1, jnp.minimum(block + 1, nw - 1), block)
                left_end = jnp.logical_and(t == 0, block == 0)
                right_end = jnp.logical_and(t == nt - 1, block == nw - 1)
                edge = jnp.where(
                    is_left,
                    edges[frame * nw + left_from].astype(jnp.float32),
                    edges[frame * nw + right_from].astype(jnp.float32),
                )
                edge = silu_of_double((edge - norm_edge[0]) * norm_edge[1] + norm_edge[2])
                raw = blocks[j, r].astype(jnp.float32)
                middle = silu_of_double((raw - norm[0:1, :]) * norm[1:2, :] + norm[2:3, :])
                sides = [
                    jnp.where(r == 0, edge[4 * k : 4 * k + 3], edge[4 * k + 1 : 4 * k + 4]) for k in range(blocks_of)
                ]
                left = jnp.concatenate([piece[0:1] for piece in sides], axis=1)
                right = jnp.concatenate([piece[2:3] for piece in sides], axis=1)
                left = jnp.where(left_end, middle[0:1, :], left)
                right = jnp.where(right_end, middle[part - 1 : part, :], right)
                before = pltpu.roll(middle, 1, 0)
                before = jnp.concatenate([jnp.where(first, left, before[0:8]), before[8:]], axis=0)
                after = pltpu.roll(middle, part - 1, 0)
                after = jnp.concatenate([after[: part - 8], jnp.where(last, right, after[part - 8 :])], axis=0)
                place = pl.ds(pl.multiple_of(block * part, part), part)
                acts[r, frame, place, 0:channels] = before.astype(jnp.bfloat16)
                acts[r, frame, place, channels : 2 * channels] = middle.astype(jnp.bfloat16)
                acts[r, frame, place, 2 * channels : 3 * channels] = after.astype(jnp.bfloat16)
            return carry

        lax.fori_loop(0, plane // 4, step, 0)

    def product(r, frames, taps):
        window = acts[r, 0:frames].reshape(frames * span, depth)
        return jnp.dot(window, taps, preferred_element_type=jnp.float32).reshape(frames, span, taps.shape[1])

    def rim(side):
        early = product(side, nt - 1, rim_pair[side])
        third_tap = product(side, nt, rim_last[side])
        first_tap, second_tap = early[:, :, 0:LANES], early[:, :, LANES:]
        for frame in range(nt):
            total = first_tap[max(frame - 2, 0)] + second_tap[max(frame - 1, 0)] + third_tap[frame]
            rim_out[side, frame] = total.astype(jnp.bfloat16)
        at_end = h == jnp.where(side == 0, 0, nh - 1)

        @pl.when(at_end)
        def _():
            rim_in[side] = rim_out[side]

        @pl.when(jnp.logical_not(at_end))
        def _():
            pltpu.make_async_remote_copy(
                src_ref=rim_out.at[side], dst_ref=rim_in.at[1 - side],
                send_sem=rim_send.at[side], recv_sem=rim_recv.at[1 - side],
                device_id=(t, h - 1 + 2 * side, w), device_id_type=MESH,
            ).start()

    for stage in range(2):
        r = across if stage == 0 else 1 - across
        all_arrived(blocks.at[others, 0], 1 + stage)
        if stage == 0:
            own_block.wait()
            all_arrived(edges.at[others], 7)
        activate(r)
        rim(r)

        for k in range(3):
            made = product(r, nt - 2 + k, pairs[r, k])
            for frame in range(nt):
                part_sum = made[max(frame - 2 + k, 0)]
                acc[frame] = part_sum if stage == 0 and k == 0 else acc[frame] + part_sum

    for side in range(2):
        at_end = (h == 0) if side == 0 else (h == nh - 1)

        @pl.when(jnp.logical_not(at_end))
        def _(side=side):
            pltpu.make_async_copy(rim_in.at[side], rim_in.at[side], rim_recv.at[side]).wait()
            pltpu.make_async_copy(rim_out.at[side], rim_out.at[side], rim_send.at[side]).wait()

    pivot = acc[0, 0:1, 0:LANES] + rim_in[0, 0, 0:16].astype(jnp.float32)[0:1]
    sums = jnp.zeros((1, LANES), jnp.float32)
    squares = jnp.zeros((1, LANES), jnp.float32)
    for r in range(2):
        total = acc[:, :, r * LANES : (r + 1) * LANES] + rim_in[r].astype(jnp.float32)
        conv_out[r] = total.astype(jnp.bfloat16)
        moved = total.reshape(rows, LANES) - pivot
        sums = sums + jnp.sum(moved, axis=0, keepdims=True)
        squares = squares + jnp.sum(moved * moved, axis=0, keepdims=True)
    mean = pivot + sums / (2 * rows)
    deviation = jnp.maximum(squares - sums * (sums / (2 * rows)), 0.0)
    line_two[h] = jnp.zeros((8, LANES), jnp.float32)
    group_mean, group_deviation = grouped_terms(
        jnp.broadcast_to(mean, (8, LANES)), jnp.broadcast_to(deviation, (8, LANES)), float(2 * rows), float(width)
    )
    line_two[h, 0:1, :] = group_mean[0:1]
    line_two[h, 1:2, :] = group_deviation[0:1]
    line_loop(lambda j: remote(line_two.at[h], line_two.at[h], 4, (t, j, w)).start())

    def result_of(frame, block):
        return conv_out.at[:, frame, pl.ds(pl.multiple_of(block * part, part), part), :]

    own_place = back.at[:, pl.ds(t * part, part), pl.ds(pl.multiple_of(w * LANES, LANES), LANES)]
    for offset in far_first:
        y, q = plane_peer(offset)
        remote(result_of(y, q), own_place, 5, (y, h, q)).start()
    own_back = pltpu.make_async_copy(result_of(t, w), own_place, local_sem.at[0])
    own_back.start()

    all_arrived(line_two.at[pl.ds(0, nh - 1)], 4)
    mean, deviation = combined(line_two[:, 0:1, :], line_two[:, 1:2, :], float(2 * rows * width), 0)
    plane_two[me] = jnp.zeros((8, LANES), jnp.float32)
    plane_two[me, 0:1, :] = mean
    plane_two[me, 1:2, :] = deviation
    for offset in far_first:
        y, q = plane_peer(offset)
        remote(plane_two.at[me], plane_two.at[me], 6, (y, h, q)).start()
    all_sent(plane_one.at[others], 0)
    all_sent(edges.at[others], 7)
    all_sent(blocks.at[others, 0], 1)
    all_sent(blocks.at[others, 0], 2)
    all_sent(line_one.at[pl.ds(0, nh - 1)], 3)
    all_sent(line_two.at[pl.ds(0, nh - 1)], 4)
    all_sent(blocks.at[others, :, :, 0:LANES], 5)
    all_arrived(blocks.at[others, :, :, 0:LANES], 5)
    own_back.wait()
    all_arrived(plane_two.at[others], 6)
    gathered = plane_two[...].reshape(nt, nw, 8, LANES)
    mean, deviation = combined(gathered[:, :, 0, :], gathered[:, :, 1, :], float(2 * rows * nh * width), 0)
    inverse = lax.rsqrt(deviation / float(everywhere * width) + EPS)
    mean_two[...] = jnp.concatenate(lane_blocks(mean), axis=1)
    scale_two[...] = jnp.concatenate(lane_blocks(inverse), axis=1) * (0.5 * gain_two[...])
    half_shift[...] = 0.5 * shift_two[...]
    all_sent(plane_two.at[others], 6)


def solution(mesh):
    nt, nh, nw = mesh.shape["tm"], mesh.shape["ha"], mesh.shape["wa"]

    def per_device(features, gain_one, shift_one, conv_weight, gain_two, shift_two):
        columns, channels = features.shape[2], features.shape[3]
        own = conv_weight.shape[4]
        plane, part, depth = nt * nw, columns // nt, 3 * channels
        span = nw * part
        rows = nt * span
        vmem = pl.BlockSpec(memory_space=pltpu.VMEM)
        bf16, f32 = jnp.bfloat16, jnp.float32
        back, mean, scale, shift = pl.pallas_call(
            functools.partial(kernel, nt, nh, nw),
            out_shape=(pltpu.VMEM((2, columns, channels), bf16), *[pltpu.VMEM((1, channels), f32)] * 3),
            in_specs=[pl.BlockSpec(memory_space=pltpu.HBM)] * 6,
            out_specs=(vmem,) * 4,
            scratch_shapes=[
                pltpu.VMEM(features.shape, bf16),
                pltpu.VMEM((1, channels), f32),
                pltpu.VMEM((1, channels), f32),
                pltpu.VMEM((1, channels), f32),
                pltpu.VMEM((1, channels), f32),
                pltpu.VMEM((nt, 16, LANES), bf16),
                pltpu.VMEM((plane, 2, part, channels), bf16),
                pltpu.VMEM((plane, 16, LANES), bf16),
                pltpu.VMEM((2, nt, span, depth), bf16),
                pltpu.VMEM((2, 3, depth, 2 * own), bf16),
                pltpu.VMEM((2, depth, 2 * own), bf16),
                pltpu.VMEM((2, depth, own), bf16),
                pltpu.VMEM((nt, span, 2 * own), f32),
                pltpu.VMEM((2, nt, span, own), bf16),
                pltpu.VMEM((2, nt, span, own), bf16),
                pltpu.VMEM((2, nt, span, own), bf16),
                pltpu.VMEM((plane, 8, LANES), f32),
                pltpu.VMEM((nh, 8, LANES), f32),
                pltpu.VMEM((nh, 8, LANES), f32),
                pltpu.VMEM((plane, 8, LANES), f32),
                pltpu.VMEM((8, channels), f32),
                pltpu.VMEM((3, 16, LANES), f32),
                pltpu.SemaphoreType.DMA((5,)),
                pltpu.SemaphoreType.DMA((18,)),
                pltpu.SemaphoreType.DMA((1,)),
                pltpu.SemaphoreType.DMA((8,)),
                pltpu.SemaphoreType.DMA((8,)),
                pltpu.SemaphoreType.DMA((2,)),
                pltpu.SemaphoreType.DMA((2,)),
            ],
            compiler_params=pltpu.CompilerParams(
                collective_id=0, has_side_effects=True, vmem_limit_bytes=60 * 1024 * 1024
            ),
        )(
            features,
            gain_one.reshape(1, channels),
            shift_one.reshape(1, channels),
            conv_weight.reshape(3, 3, depth, own),
            gain_two.reshape(1, channels),
            shift_two.reshape(1, channels),
        )
        result = silu_of_double((back.astype(f32) - mean) * scale + shift)
        return result.astype(bf16)[None]

    in_specs = (P("tm", "ha", "wa", None), P(), P(), P(None, None, None, None, "wa"), P(), P())
    return jax.shard_map(
        per_device, mesh=mesh, in_specs=in_specs, out_specs=P("tm", "ha", "wa", None), check_vma=False
    )
```
